512 devices in a mesh: dom: 256 (over x, z, y), band: 2 (over core).
Axes of the slice: x: 4, y: 8, z: 8, core: 2. Of those that a mesh axis runs over, the one named last changes fastest.
Arguments:
- trial_block: float32 [32, 2048, 8, 128], P('band', 'dom'), may hold values from -18 to 18
- potential: float32 [2048, 8, 128], P('dom'), may hold values from -3 to 1
Outputs:
- orbitals: float32 [32, 2048, 8, 128], P('band', 'dom')
- projected: float32 [32, 32], replicated
The draws below stay inside these ranges and needn't reach their ends.
All inputs are finite; a program needn't handle non-finite values.
Results may differ from the reference program's by a relative error of at most 0.0003.
Values sent between devices are 32-bit elements; how exact they have to be, the bound alone decides.
A program may use at most 64 MiB of HBM per device.

```python
import jax
import jax.numpy as jnp
from jax import lax

BANDS = 32
DEGREE = 4
NY = 8
NZ = 128
NX = 2048


def draw_trial_block(key, part):
    envelope = 1.0 + 2.0 * jnp.arange(NX, dtype=jnp.float32) / (NX - 1)
    envelope = envelope[None, :, None, None]
    block_shape = (BANDS, NX, NY, NZ)
    values = jnp.clip(jax.random.normal(key, block_shape), -6.0, 6.0)
    return (envelope * values).astype(jnp.float32)


def level_of(stream_key, extent, cuts, least, top_value):
    gain = 1.0
    for axis_at, shards_of in cuts:
        heights = jax.random.uniform(jax.random.fold_in(jax.random.fold_in(stream_key, 6), axis_at), (shards_of,), jnp.float32, least / len(cuts), top_value / len(cuts))
        gain = gain * jnp.repeat(jnp.exp(heights), extent[axis_at] // shards_of).reshape((-1,) + (1,) * (len(extent) - 1 - axis_at))
    return gain


def setup_inputs(seed: int = 0) -> dict:
    seeds = jax.random.split(jax.random.key(seed), 3)
    return {
        "trial_block": draw_trial_block(jax.random.fold_in(seeds[2], 71), 0),
        "potential": jnp.clip(-3.0 + 4.0 * jax.random.uniform(seeds[1], (NX, NY, NZ), jnp.float32) ** level_of(seeds[1], (NX, NY, NZ), ((0, 256),), -0.2, 0.2), -3.0, 1.0),
    }


COEFFS = (-205.0 / 72.0, 8.0 / 5.0, -1.0 / 5.0, 8.0 / 315.0, -1.0 / 560.0)
CENTER = 5.75
HALF_WIDTH = 5.25

def axis_second(field, axis):
    length = field.shape[axis]
    widths = [(0, 0)] * field.ndim
    widths[axis] = (4, 4)
    padded = jnp.pad(field, widths)
    summed = COEFFS[0] * field
    for offset in range(1, 5):
        upper = lax.slice_in_dim(padded, 4 + offset, 4 + offset + length, axis=axis)
        below = lax.slice_in_dim(padded, 4 - offset, 4 - offset + length, axis=axis)
        summed = summed + COEFFS[offset] * (upper + below)
    return summed

def hamiltonian(field, potential):
    lap = axis_second(field, 0) + axis_second(field, 1) + axis_second(field, 2)
    return -0.5 * lap + potential * field

def chebyshev(start, potential):
    previous = start
    current = (hamiltonian(start, potential) - CENTER * start) / HALF_WIDTH
    for step in range(DEGREE - 1):
        following = 2.0 * (hamiltonian(current, potential) - CENTER * current) / HALF_WIDTH - previous
        previous, current = (current, following)
    return current

def reference(trial_block, potential):
    filtered = lax.map(lambda band: chebyshev(band, potential), trial_block)
    flat = filtered.reshape(BANDS, -1)
    cell_count = flat.shape[1]
    gram = jnp.dot(flat, flat.T, precision=lax.Precision.HIGHEST) / cell_count
    lower = jnp.linalg.cholesky(gram)
    inverse = lax.linalg.triangular_solve(lower, jnp.eye(BANDS, dtype=gram.dtype), left_side=True, lower=True)
    ortho = jnp.dot(inverse, flat, precision=lax.Precision.HIGHEST)
    orbitals = ortho.reshape(trial_block.shape)
    images = lax.map(lambda band: hamiltonian(band, potential), orbitals)
    projected = jnp.dot(ortho, images.reshape(BANDS, -1).T, precision=lax.Precision.HIGHEST) / cell_count
    return (orbitals, projected)
```

```python
import functools

import jax
import jax.numpy as jnp
from jax import lax
from jax.experimental import pallas as pl
from jax.experimental.pallas import tpu as pltpu
from jax.sharding import PartitionSpec as P

COEFFS = (-205.0 / 72.0, 8.0 / 5.0, -1.0 / 5.0, 8.0 / 315.0, -1.0 / 560.0)
CENTER = 5.75
HALF_WIDTH = 5.25
DEGREE = 4

PAIR = tuple(-0.5 * c / HALF_WIDTH for c in COEFFS)
DIAG = -1.5 * COEFFS[0] - CENTER

MESH = pl.DeviceIdType.MESH
NT = (((1,), (1,)), ((), ()))
NN = (((1,), (0,)), ((), ()))
RINGS = {256: (4, 8, 8), 8: (2, 2, 2)}


def far_first(count):
    return sorted(range(1, count), key=lambda d: -min(d, count - d))


def kernel(
    rings,
    trial,
    potential,
    orbitals,
    projected,
    nat,
    pot,
    weight,
    field,
    halo,
    other,
    split,
    usplit,
    tile,
    slots,
    in_sem,
    halo_send,
    halo_recv,
    sib_send,
    sib_recv,
    red_send,
    red_recv,
):
    nx, nz, ny = rings
    doms = nx * nz * ny
    cells = doms * 8 * 8 * 128
    dom = lax.axis_index("dom")
    band = lax.axis_index("band")
    py = lax.rem(dom, ny)
    pz = lax.rem(lax.div(dom, ny), nz)
    px = lax.div(dom, ny * nz)
    left = lax.rem(dom + doms - 1, doms)
    right = lax.rem(dom + 1, doms)

    def at(x, z, y):
        return (x * nz + z) * ny + y

    def member_y(p):
        return {"dom": at(px, pz, p), "band": band}

    def member_z(p):
        return {"dom": at(px, p, py), "band": band}

    def member_x(p):
        return {"dom": at(lax.div(p, 2), pz, py), "band": lax.rem(p, 2)}

    phases = ((ny, py, member_y), (nz, pz, member_z), (2 * nx, 2 * px + band, member_x))

    loads = [
        pltpu.make_async_copy(potential, pot, in_sem.at[2]),
        pltpu.make_async_copy(trial.at[pl.ds(0, 512)], nat.at[pl.ds(0, 512)], in_sem.at[0]),
        pltpu.make_async_copy(trial.at[pl.ds(512, 512)], nat.at[pl.ds(512, 512)], in_sem.at[1]),
    ]
    for load in loads:
        load.start()

    barrier = pltpu.get_barrier_semaphore()
    greeted = 0
    for count, place, member in phases:
        for d in far_first(count):
            pl.semaphore_signal(
                barrier, inc=1, device_id=member(lax.rem(place + d, count)), device_id_type=MESH
            )
            greeted += 1
    for neighbour in (left, right):
        pl.semaphore_signal(
            barrier, inc=1, device_id={"dom": neighbour, "band": band}, device_id_type=MESH
        )
        greeted += 1

    zeros = jnp.zeros((4, 8, 8, 128), jnp.float32)

    def clear(i, carry):
        s, g = lax.div(i, 2), lax.rem(i, 2)
        field[s, g, pl.ds(0, 4)] = zeros
        field[s, g, pl.ds(12, 4)] = zeros
        return carry

    lax.fori_loop(0, 2 * (DEGREE + 1), clear, 0)

    loads[0].wait()

    def set_weight(x, carry):
        rows = (pot[x] + DIAG) * (1.0 / HALF_WIDTH)
        for y in range(8):
            weight[x, y] = jnp.broadcast_to(rows[y : y + 1], (8, 128))
        return carry

    lax.fori_loop(0, 8, set_weight, 0)

    def relayout(g):
        def body(x, carry):
            for y in range(8):
                field[0, g, 4 + x, y] = nat[pl.ds(g * 512 + x * 8 + y, 8, stride=64), :]
            return carry

        lax.fori_loop(0, 8, body, 0)

    def halo_copy(s, g, side):
        width = 4 if s < DEGREE else 2
        first = 12 - width if side == 0 else 4
        land = 4 - width if side == 0 else 0
        return pltpu.make_async_remote_copy(
            src_ref=field.at[s, g, pl.ds(first, width)],
            dst_ref=halo.at[s, g, side, pl.ds(land, width)],
            send_sem=halo_send.at[s, g, side],
            recv_sem=halo_recv.at[s, g, side],
            device_id={"dom": right if side == 0 else left, "band": band},
            device_id_type=MESH,
        )

    lane = lax.broadcasted_iota(jnp.int32, (8, 8, 128), 2)

    def shifted_y(c, k):
        empty = jnp.zeros((k, 8, 128), jnp.float32)
        return jnp.concatenate([c[k:], empty], 0) + jnp.concatenate([empty, c[: 8 - k]], 0)

    def shifted_z(c, k):
        below = jnp.where(lane >= k, pltpu.roll(c, k, 2), 0.0)
        return below + jnp.where(lane < 128 - k, pltpu.roll(c, 128 - k, 2), 0.0)

    def local_part(s, g):
        def body(x, carry):
            c = field[s, g, 4 + x]
            total = weight[x] * c
            for k in range(1, 5):
                pairs = field[s, g, 4 + x + k] + field[s, g, 4 + x - k]
                pairs = pairs + shifted_y(c, k) + shifted_z(c, k)
                total = total + PAIR[k] * pairs
            if 1 <= s < DEGREE:
                total = 2.0 * total - field[s - 1, g, 4 + x]
            field[s + 1, g, 4 + x] = total
            return carry

        lax.fori_loop(0, 8, body, 0)

    def halo_part(s, g, side):
        twice = 1.0 if s == 0 else 2.0
        for x in range(4):
            mine = 4 + x if side == 0 else 11 - x
            total = field[s + 1, g, mine]
            for layer in range(1, 5 - x):
                if s == DEGREE and (layer > 2 or (side == 1 and x < 2)):
                    continue
                theirs = 4 - layer if side == 0 else layer - 1
                total = total + (twice * PAIR[x + layer]) * halo[s, g, side, theirs]
            field[s + 1, g, mine] = total

    def add_halo(s, g, side):
        halo_copy(s, g, side).wait_recv()
        has = dom > 0 if side == 0 else dom < doms - 1

        @pl.when(has)
        def _():
            halo_part(s, g, side)

    def sibling_copy(g):
        return pltpu.make_async_remote_copy(
            src_ref=field.at[DEGREE, g, pl.ds(4, 8)],
            dst_ref=other.at[g],
            send_sem=sib_send.at[g],
            recv_sem=sib_recv.at[g],
            device_id={"dom": dom, "band": 1 - band},
            device_id_type=MESH,
        )

    def reduce_copy(m, f, d):
        count, place, member = phases[f]
        return pltpu.make_async_remote_copy(
            src_ref=slots.at[m, f, place],
            dst_ref=slots.at[m, f, place],
            send_sem=red_send.at[m, f, d],
            recv_sem=red_recv.at[m, f, place],
            device_id=member(lax.rem(place + d, count)),
            device_id_type=MESH,
        )

    def reduce_start(m, f, value):
        count, place, _ = phases[f]
        slots[m, f, place] = value
        for d in far_first(count):
            reduce_copy(m, f, d).start()

    def reduce_wait(m, f):
        count, place, member = phases[f]
        for d in range(1, count):
            source = lax.rem(place + d, count)
            pltpu.make_async_remote_copy(
                src_ref=slots.at[m, f, source],
                dst_ref=slots.at[m, f, source],
                send_sem=red_send.at[m, f, d],
                recv_sem=red_recv.at[m, f, source],
                device_id=member(source),
                device_id_type=MESH,
            ).wait_recv()

    def reduced(m, f):
        reduce_wait(m, f)
        total = slots[m, f, 0]
        for p in range(1, phases[f][0]):
            total = total + slots[m, f, p]
        return total

    def split_rows(value):
        high = value.astype(jnp.bfloat16)
        return high, (value - high.astype(jnp.float32)).astype(jnp.bfloat16)

    def split_own(target, s, first, low):
        def body(x, carry):
            for y in range(8):
                value = jnp.concatenate([field[s, 0, 4 + x, y], field[s, 1, 4 + x, y]], 0)
                hi, lo = split_rows(value)
                cols = pl.ds((y % 2) * 128, 128)
                target[x * 4 + y // 2, pl.ds(first, 16), cols] = hi
                target[x * 4 + y // 2, pl.ds(low + first, 16), cols] = lo
            return carry

        lax.fori_loop(0, 8, body, 0)

    def split_other(first):
        def body(x, carry):
            for y in range(8):
                hi, lo = split_rows(jnp.concatenate([other[0, x, y], other[1, x, y]], 0))
                cols = pl.ds((y % 2) * 128, 128)
                split[x * 4 + y // 2, pl.ds(first, 16), cols] = hi
                split[x * 4 + y // 2, pl.ds(32 + first, 16), cols] = lo
            return carry

        lax.fori_loop(0, 8, body, 0)

    own_rows = pl.multiple_of(band * 16, 16)
    other_rows = pl.multiple_of(16 - band * 16, 16)

    def products(left_of):
        def body(i, total):
            for j in range(4):
                total = total + lax.dot_general(
                    left_of(i * 4 + j), split[i * 4 + j], NT, preferred_element_type=jnp.float32
                )
            return total

        total = lax.fori_loop(0, 8, body, jnp.zeros((32, 64), jnp.float32))
        total = total[:16] + total[16:]
        tile[:, pl.ds(0, 64)] = total[:8]
        tile[:, pl.ds(64, 64)] = total[8:]
        return tile[...]

    def own_split(i):
        return jnp.concatenate(
            [split[i, pl.ds(own_rows, 16)], split[i, pl.ds(32 + own_rows, 16)]], 0
        )

    def unpacked(m):
        reduce_wait(m, 2)
        rows = []
        for core in range(2):
            total = slots[m, 2, core]
            for p in range(1, nx):
                total = total + slots[m, 2, 2 * p + core]
            total = total + pltpu.roll(total, 96, 1)
            rows += [total, pltpu.roll(total, 64, 1)]
        return rows

    pl.semaphore_wait(barrier, greeted)

    started = []

    def start(copy):
        copy.start()
        started.append(copy)

    for g in range(2):
        loads[1 + g].wait()
        relayout(g)
        for side in range(2):
            start(halo_copy(0, g, side))
    for g in range(2):
        local_part(0, g)
    for s in range(DEGREE):
        for g in range(2):
            for side in range(2):
                add_halo(s, g, side)
                if s + 1 < DEGREE:
                    start(halo_copy(s + 1, g, 1 - side))
            if s + 1 < DEGREE:
                local_part(s + 1, g)
            else:
                start(sibling_copy(g))
                for side in range(2):
                    start(halo_copy(DEGREE, g, side))

    split_own(split, DEGREE, own_rows, 32)
    for g in range(2):
        sibling_copy(g).wait_recv()
    split_other(other_rows)
    reduce_start(0, 0, products(own_split))
    for g in range(2):
        local_part(DEGREE, g)
    reduce_start(0, 1, reduced(0, 0))
    for g in range(2):
        for side in range(2):
            add_halo(DEGREE, g, side)
    split_own(usplit, DEGREE + 1, 0, 16)
    reduce_start(0, 2, reduced(0, 1))
    reduce_start(1, 0, products(lambda i: usplit[i]))

    lanes = lax.broadcasted_iota(jnp.int32, (8, 128), 1)
    subs = lax.broadcasted_iota(jnp.int32, (8, 128), 0)
    gram = [jnp.where(lanes < 32, r, 0.0) * (1.0 / cells) for r in unpacked(0)]
    rows = [
        jnp.where(lanes == subs + (32 + 8 * q), 1.0, gram[q]) for q in range(4)
    ]
    scale = [jnp.zeros((8, 128), jnp.float32) for _ in range(4)]
    for j in range(32):
        r, s = divmod(j, 8)
        row = jnp.broadcast_to(rows[r][s : s + 1], (8, 128))
        pivot = jnp.broadcast_to(row[:, j : j + 1], (8, 128))
        scale[r] = jnp.where(subs == s, pivot, scale[r])
        row = row / pivot
        for q in range(r, 4):
            new = rows[q] - jnp.broadcast_to(rows[q][:, j : j + 1], (8, 128)) * row
            rows[q] = jnp.where(subs > s, new, rows[q]) if q == r else new
    inverse = [
        jnp.where(lanes < 32, pltpu.roll(rows[q] * lax.rsqrt(scale[q]), 96, 1), 0.0)
        for q in range(4)
    ]

    own = [jnp.where(band == 0, inverse[q], inverse[2 + q]) for q in range(2)]
    own = jnp.concatenate([v + pltpu.roll(v, 32, 1) for v in own], 0)
    hi, lo = split_rows(own)
    own = jnp.concatenate([hi, lo], 0)[:, :64]

    def combine(x, carry):
        for y in range(0, 8, 2):
            value = lax.dot_general(
                own, split[x * 4 + y // 2], NN, preferred_element_type=jnp.float32
            )
            value = value[:16] + value[16:]
            nat[pl.ds(x * 8 + y, 16, stride=64), :] = value[:, :128]
            nat[pl.ds(x * 8 + y + 1, 16, stride=64), :] = value[:, 128:]
        return carry

    lax.fori_loop(0, 8, combine, 0)
    out = pltpu.make_async_copy(nat, orbitals, in_sem.at[0])
    out.start()

    reduce_start(1, 1, reduced(1, 0))
    reduce_start(1, 2, reduced(1, 1))
    image = [
        (HALF_WIDTH / cells) * i + CENTER * g for i, g in zip(unpacked(1), gram)
    ]
    image = jnp.concatenate(image, 0)[:, :32]
    inverse = jnp.concatenate(inverse, 0)[:, :32]
    dot = functools.partial(
        lax.dot_general, precision=lax.Precision.HIGHEST, preferred_element_type=jnp.float32
    )
    both = dot(inverse, image, NN) + dot(inverse, image, NT)
    projected[...] = 0.5 * dot(both, inverse, NT)

    for copy in started:
        copy.wait_send()
    for m in range(2):
        for f in range(3):
            for d in range(1, phases[f][0]):
                reduce_copy(m, f, d).wait_send()
    out.wait()


def shards(trial_block, potential):
    rings = RINGS[lax.axis_size("dom")]
    most = max(rings[1], rings[2], 2 * rings[0])
    f32, dma = jnp.float32, pltpu.SemaphoreType.DMA
    orbitals, projected = pl.pallas_call(
        functools.partial(kernel, rings),
        out_shape=(
            jax.ShapeDtypeStruct((1024, 128), f32),
            jax.ShapeDtypeStruct((32, 32), f32),
        ),
        in_specs=[pl.BlockSpec(memory_space=pl.ANY)] * 2,
        out_specs=(
            pl.BlockSpec(memory_space=pl.ANY),
            pl.BlockSpec(memory_space=pltpu.VMEM),
        ),
        scratch_shapes=[
            pltpu.VMEM((1024, 128), f32),
            pltpu.VMEM((8, 8, 128), f32),
            pltpu.VMEM((8, 8, 8, 128), f32),
            pltpu.VMEM((DEGREE + 2, 2, 16, 8, 8, 128), f32),
            pltpu.VMEM((DEGREE + 1, 2, 2, 4, 8, 8, 128), f32),
            pltpu.VMEM((2, 8, 8, 8, 128), f32),
            pltpu.VMEM((32, 64, 256), jnp.bfloat16),
            pltpu.VMEM((32, 32, 256), jnp.bfloat16),
            pltpu.VMEM((8, 128), f32),
            pltpu.VMEM((2, 3, most, 8, 128), f32),
            dma((3,)),
            dma((DEGREE + 1, 2, 2)),
            dma((DEGREE + 1, 2, 2)),
            dma((2,)),
            dma((2,)),
            dma((2, 3, most)),
            dma((2, 3, most)),
        ],
        compiler_params=pltpu.CompilerParams(
            collective_id=0, has_side_effects=True, vmem_limit_bytes=40 * 1024 * 1024
        ),
        cost_estimate=pl.CostEstimate(
            flops=200_000_000, bytes_accessed=1_100_000, transcendentals=0
        ),
    )(trial_block.reshape(1024, 128), potential)
    return orbitals.reshape(trial_block.shape), projected


def solution(mesh):
    return jax.shard_map(
        shards,
        mesh=mesh,
        in_specs=(P("band", "dom", None, None), P("dom", None, None)),
        out_specs=(P("band", "dom", None, None), P()),
        check_vma=False,
    )
```

```python
import functools

import jax
import jax.numpy as jnp
from jax import lax
from jax.experimental import pallas as pl
from jax.experimental.pallas import tpu as pltpu
from jax.sharding import PartitionSpec as P

COEFFS = (-205.0 / 72.0, 8.0 / 5.0, -1.0 / 5.0, 8.0 / 315.0, -1.0 / 560.0)
CENTER = 5.75
HALF_WIDTH = 5.25
DEGREE = 4

PAIR = tuple(-0.5 * c / HALF_WIDTH for c in COEFFS)
DIAG = -1.5 * COEFFS[0] - CENTER

MESH = pl.DeviceIdType.MESH
NT = (((1,), (1,)), ((), ()))
NN = (((1,), (0,)), ((), ()))
PARTS = 4
YS = 8 // PARTS
SHIFT = (0, 8, 64, 72)
SUMS = ((0, 0), (0, 1), (1, 0), (1, 1), (1, 2))
RINGS = {256: (4, 8, 8), 8: (2, 2, 2)}


def far_first(count):
    return sorted(range(1, count), key=lambda d: -min(d, count - d))


def kernel(
    rings,
    trial,
    potential,
    orbitals,
    projected,
    nat,
    pot,
    pot_far,
    weight,
    weight_far,
    field,
    halo,
    far,
    other,
    split,
    usplit,
    tile,
    slots,
    in_sem,
    halo_send,
    halo_recv,
    far_send,
    far_recv,
    sib_send,
    sib_recv,
    red_send,
    red_recv,
):
    nx, nz, ny = rings
    doms = nx * nz * ny
    cells = doms * 8 * 8 * 128
    dom = lax.axis_index("dom")
    band = lax.axis_index("band")
    py = lax.rem(dom, ny)
    pz = lax.rem(lax.div(dom, ny), nz)
    px = lax.div(dom, ny * nz)
    left = lax.rem(dom + doms - 1, doms)
    right = lax.rem(dom + 1, doms)

    def at(x, z, y):
        return (x * nz + z) * ny + y

    pairs = nx // 2
    half = lax.div(px, 2)

    def member_yx(p):
        x = 2 * half + lax.rem(p, 2)
        return {"dom": at(x, pz, lax.div(p, 2)), "band": band}

    def member_zx(p):
        x = jnp.where(lax.rem(p, pairs) == half, px, nx - 1 - px)
        return {"dom": at(x, lax.div(p, pairs), py), "band": band}

    def member_core(p):
        return {"dom": dom, "band": p}

    phases = (
        (2 * ny, 2 * py + lax.rem(px, 2), member_yx),
        (pairs * nz, pairs * pz + half, member_zx),
        (2, band, member_core),
    )

    loads = [
        pltpu.make_async_copy(potential, pot, in_sem.at[2]),
        pltpu.make_async_copy(trial.at[pl.ds(0, 512)], nat.at[pl.ds(0, 512)], in_sem.at[0]),
        pltpu.make_async_copy(trial.at[pl.ds(512, 512)], nat.at[pl.ds(512, 512)], in_sem.at[1]),
    ]
    for load in loads:
        load.start()

    barrier = pltpu.get_barrier_semaphore()
    greeted = 0
    for count, place, member in phases:
        for d in far_first(count):
            pl.semaphore_signal(
                barrier, inc=1, device_id=member(lax.rem(place + d, count)), device_id_type=MESH
            )
            greeted += 1
    for neighbour in (left, right):
        pl.semaphore_signal(
            barrier, inc=1, device_id={"dom": neighbour, "band": band}, device_id_type=MESH
        )
        greeted += 1

    zeros = jnp.zeros((4, 8, 8, 128), jnp.float32)

    def clear(i, carry):
        s, g = lax.div(i, 2), lax.rem(i, 2)
        field[s, g, pl.ds(0, 4)] = zeros
        field[s, g, pl.ds(12, 4)] = zeros
        return carry

    def spread_weight(target, rows):
        rows = (rows + DIAG) * (1.0 / HALF_WIDTH)
        for y in range(8):
            target[y] = jnp.broadcast_to(rows[y : y + 1], (8, 128))

    def set_weight(x, carry):
        spread_weight(weight.at[x], pot[x])
        return carry

    def relayout(g):
        def body(x, carry):
            for y in range(8):
                field[0, g, 4 + x, y] = nat[pl.ds(g * 512 + x * 8 + y, 8, stride=64), :]
            return carry

        lax.fori_loop(0, 8, body, 0)

    has = (dom > 0, dom < doms - 1)

    def to_neighbour(side, src, dst, send_sem, recv_sem):
        return pltpu.make_async_remote_copy(
            src_ref=src,
            dst_ref=dst,
            send_sem=send_sem,
            recv_sem=recv_sem,
            device_id={"dom": right if side == 0 else left, "band": band},
            device_id_type=MESH,
        )

    def halo_copy(s, g, side, part):
        ys = pl.ds(part * YS, YS)
        return to_neighbour(
            side,
            field.at[s, g, pl.ds(8 if side == 0 else 4, 4), ys],
            halo.at[s, g, side, :, ys],
            halo_send.at[s, g, side, part],
            halo_recv.at[s, g, side, part],
        )

    def far_copy(g, side):
        return to_neighbour(
            side,
            field.at[last, g, pl.ds(6 if side == 0 else 8, 2)],
            far.at[g, side],
            far_send.at[g, side],
            far_recv.at[g, side],
        )

    def pot_copy(side):
        return to_neighbour(
            side,
            pot.at[pl.ds(6 if side == 0 else 0, 2)],
            pot_far.at[side],
            far_send.at[2, side],
            far_recv.at[2, side],
        )

    def send(side, copy):
        @pl.when(has[1 - side])
        def _():
            copy.start()

    lane = lax.broadcasted_iota(jnp.int32, (8, 8, 128), 2)

    def shifted_y(c, k):
        empty = jnp.zeros((k, 8, 128), jnp.float32)
        return jnp.concatenate([c[k:], empty], 0) + jnp.concatenate([empty, c[: 8 - k]], 0)

    def shifted_z(c, k):
        below = jnp.where(lane >= k, pltpu.roll(c, k, 2), 0.0)
        return below + jnp.where(lane < 128 - k, pltpu.roll(c, 128 - k, 2), 0.0)

    def local_part(s, g):
        def body(x, carry):
            c = field[s, g, 4 + x]
            total = weight[x] * c
            for k in range(1, 5):
                pairs = field[s, g, 4 + x + k] + field[s, g, 4 + x - k]
                pairs = pairs + shifted_y(c, k) + shifted_z(c, k)
                total = total + PAIR[k] * pairs
            if 1 <= s < DEGREE:
                total = 2.0 * total - field[s - 1, g, 4 + x]
            field[s + 1, g, 4 + x] = total
            return carry

        lax.fori_loop(0, 8, body, 0)

    def halo_part(s, g, side, part):
        twice = 1.0 if s == 0 else 2.0
        ys = pl.ds(part * YS, YS)
        layers = {n: halo[s, g, side, 4 - n if side == 0 else n - 1, ys] for n in range(1, 5)}
        for x in range(4):
            mine = 4 + x if side == 0 else 11 - x
            total = field[s + 1, g, mine, ys]
            for n in range(1, 5 - x):
                total = total + (twice * PAIR[x + n]) * layers[n]
            field[s + 1, g, mine, ys] = total

    def border_part(g, side):
        def cell(n):
            if n > 4:
                return far[g, side, 6 - n if side == 0 else n - 5]
            if n > 0:
                return halo[last, g, side, 4 - n if side == 0 else n - 1]
            return field[last, g, 4 - n if side == 0 else 11 + n]

        for n in (1, 2):
            c = cell(n)
            total = weight_far[side, 2 - n if side == 0 else n - 1] * c
            for k in range(1, 5):
                near = cell(n + k) + cell(n - k) + shifted_y(c, k) + shifted_z(c, k)
                total = total + PAIR[k] * near
            total = 2.0 * total - halo[last - 1, g, side, 4 - n if side == 0 else n - 1]
            for x in range(0 if side == 0 else 2, 5 - n):
                mine = 4 + x if side == 0 else 11 - x
                field[DEGREE + 1, g, mine] = field[DEGREE + 1, g, mine] + (2.0 * PAIR[x + n]) * total

    def sibling_copy(g, part):
        ys = pl.ds(part * YS, YS)
        return pltpu.make_async_remote_copy(
            src_ref=field.at[DEGREE, g, pl.ds(4, 8), ys],
            dst_ref=other.at[g, :, ys],
            send_sem=sib_send.at[g, part],
            recv_sem=sib_recv.at[g, part],
            device_id={"dom": dom, "band": 1 - band},
            device_id_type=MESH,
        )

    def reduce_copy(m, f, d):
        count, place, member = phases[f]
        return pltpu.make_async_remote_copy(
            src_ref=slots.at[m, f, place],
            dst_ref=slots.at[m, f, place],
            send_sem=red_send.at[m, f, d],
            recv_sem=red_recv.at[m, f, place],
            device_id=member(lax.rem(place + d, count)),
            device_id_type=MESH,
        )

    def reduce_start(m, f, value):
        count, place, _ = phases[f]
        slots[m, f, place] = value
        for d in far_first(count):
            reduce_copy(m, f, d).start()

    def reduce_wait(m, f):
        count, place, member = phases[f]
        for d in range(1, count):
            source = lax.rem(place + d, count)
            pltpu.make_async_remote_copy(
                src_ref=slots.at[m, f, source],
                dst_ref=slots.at[m, f, source],
                send_sem=red_send.at[m, f, d],
                recv_sem=red_recv.at[m, f, source],
                device_id=member(source),
                device_id_type=MESH,
            ).wait_recv()

    def reduced(m, f):
        reduce_wait(m, f)
        total = slots[m, f, 0]
        for p in range(1, phases[f][0]):
            total = total + slots[m, f, p]
        return total

    def split_rows(value):
        high = value.astype(jnp.bfloat16).astype(jnp.float32)
        return jnp.concatenate([high, value - high], 0).astype(jnp.bfloat16)

    def split_into(target, pair, first, read):
        def body(x, carry):
            both = [split_rows(read(x, 2 * pair + y)) for y in range(2)]
            target[x * 4 + pair, pl.ds(first, 16), :] = jnp.concatenate(both, 1)
            return carry

        lax.fori_loop(0, 8, body, 0, unroll=True)

    own_rows = pl.multiple_of(band * 32, 32)
    other_rows = pl.multiple_of(32 - band * 32, 32)

    def split_own(g, part):
        for pair in range(part * YS // 2, (part + 1) * YS // 2):
            split_into(split, pair, own_rows + 16 * g, lambda x, y: field[DEGREE, g, 4 + x, y])

    def split_other(g, part):
        for pair in range(part * YS // 2, (part + 1) * YS // 2):
            split_into(split, pair, other_rows + 16 * g, lambda x, y: other[g, x, y])

    def product(left, right):
        return lax.dot_general(left, right, NT, preferred_element_type=jnp.float32)

    def gram_part(part, total):
        for pair in range(part * YS // 2, (part + 1) * YS // 2):
            for x in range(8):
                total = total + product(split[x * 4 + pair], split[x * 4 + pair])
        return total

    def image_product():
        def body(x, total):
            for pair in range(4):
                total = total + product(usplit[x * 4 + pair], split[x * 4 + pair])
            return total

        return lax.fori_loop(0, 8, body, jnp.zeros((32, 64), jnp.float32))

    lanes = lax.broadcasted_iota(jnp.int32, (8, 128), 1)
    subs = lax.broadcasted_iota(jnp.int32, (8, 128), 0)
    used = (lanes < 64) & (lax.rem(lanes, 16) < 8)

    def folded(value):
        return value + pltpu.roll(value, 120, 1)

    def packed_gram(total):
        tile[:, pl.ds(0, 64)] = total
        value = jnp.zeros((8, 128), jnp.float32)
        for q in range(4):
            row = folded(tile[pl.ds(16 * q, 8)] + tile[pl.ds(16 * q + 8, 8)])
            row = jnp.where(used, row, 0.0)
            value = value + (row if q == 0 else pltpu.roll(row, SHIFT[q], 1))
        return value

    def unpacked_gram(value):
        rows = [value] + [pltpu.roll(value, 128 - SHIFT[q], 1) for q in range(1, 4)]
        return [jnp.where(used, row, 0.0) for row in rows]

    def packed_image(total):
        tile[pl.ds(0, 8), pl.ds(0, 64)] = total[:8] + total[8:16]
        tile[pl.ds(0, 8), pl.ds(64, 64)] = total[16:24] + total[24:]
        return tile[pl.ds(0, 8)]

    def unpacked_image():
        reduce_wait(1, 2)
        rows = []
        for core in range(2):
            total = folded(slots[1, 2, core])
            rows += [total, pltpu.roll(total, 64, 1)]
        return [jnp.where(used, row, 0.0) for row in rows]

    last = DEGREE - 1

    for g in range(2):
        loads[1 + g].wait()
        relayout(g)
        if g == 0:
            pl.semaphore_wait(barrier, greeted)
        for part in range(PARTS):
            for side in range(2):
                send(side, halo_copy(0, g, side, part))
    loads[0].wait()
    for side in range(2):
        send(side, pot_copy(side))
    lax.fori_loop(0, 2 * (DEGREE + 1), clear, 0)
    tile[...] = jnp.zeros((64, 128), jnp.float32)
    lax.fori_loop(0, 8, set_weight, 0)
    for g in range(2):
        local_part(0, g)

    for s in range(last):
        for g in range(2):

            def exchange(part, carry):
                for side in range(2):

                    @pl.when(has[side])
                    def _():
                        halo_copy(s, g, side, part).wait_recv()
                        halo_part(s, g, side, part)
                        halo_copy(s + 1, g, 1 - side, part).start()

                return carry

            lax.fori_loop(0, PARTS, exchange, 0)
            local_part(s + 1, g)
    for g in range(2):
        for side in range(2):
            send(side, far_copy(g, side))

    for side in range(2):

        @pl.when(has[side])
        def _():
            pot_copy(side).wait_recv()
            for n in range(2):
                spread_weight(weight_far.at[side, n], pot_far[side, n])

    gram = jnp.zeros((64, 64), jnp.float32)
    for g in range(2):
        for part in range(PARTS):
            for side in range(2):

                @pl.when(has[side])
                def _():
                    halo_copy(last, g, side, part).wait_recv()
                    halo_part(last, g, side, part)

            sibling_copy(g, part).start()
            split_own(g, part)
            if part > 0:
                sibling_copy(g, part - 1).wait_recv()
                split_other(g, part - 1)
                if g == 1:
                    gram = gram_part(part - 1, gram)
        if g == 0:
            local_part(DEGREE, 0)
        sibling_copy(g, PARTS - 1).wait_recv()
        split_other(g, PARTS - 1)
    reduce_start(0, 0, packed_gram(gram_part(PARTS - 1, gram)))

    local_part(DEGREE, 1)
    for side in range(2):

        @pl.when(has[side])
        def _():
            for g in range(2):
                far_copy(g, side).wait_recv()
                border_part(g, side)

    for g in range(2):
        for pair in range(4):
            split_into(usplit, pair, 16 * g, lambda x, y: field[DEGREE + 1, g, 4 + x, y])
    reduce_start(1, 0, packed_image(image_product()))
    reduce_start(0, 1, reduced(0, 0))
    reduce_start(1, 1, reduced(1, 0))

    gram = [row * (1.0 / cells) for row in unpacked_gram(reduced(0, 1))]
    rows = [jnp.where(lanes == subs + (64 + 16 * q), 1.0, gram[q]) for q in range(4)]
    inverse = eliminated(rows, subs)
    inverse = [jnp.where(used, pltpu.roll(row, 64, 1), 0.0) for row in inverse]

    reduce_start(1, 2, reduced(1, 1))
    own = [jnp.where(band == 0, inverse[q], inverse[2 + q]) for q in range(2)]
    own = split_rows(jnp.concatenate([v + pltpu.roll(v, 8, 1) for v in own], 0))[:, :64]

    def combine(x, carry):
        for y in range(0, 8, 2):
            value = lax.dot_general(
                own, split[x * 4 + y // 2], NN, preferred_element_type=jnp.float32
            )
            value = value[:16] + value[16:]
            nat[pl.ds(x * 8 + y, 16, stride=64), :] = value[:, :128]
            nat[pl.ds(x * 8 + y + 1, 16, stride=64), :] = value[:, 128:]
        return carry

    lax.fori_loop(0, 8, combine, 0)
    out = pltpu.make_async_copy(nat, orbitals, in_sem.at[0])
    out.start()

    dot = functools.partial(
        lax.dot_general, precision=lax.Precision.HIGHEST, preferred_element_type=jnp.float32
    )
    inverse = jnp.concatenate(inverse, 0)[:, :64]
    column = lax.broadcasted_iota(jnp.int32, (64, 32), 1)
    spread = lax.broadcasted_iota(jnp.int32, (64, 32), 0)
    spread = spread == 16 * lax.div(column, 8) + lax.rem(column, 8)
    narrow = dot(inverse, jnp.where(spread, 1.0, 0.0), NN)
    image = [(HALF_WIDTH / cells) * i + CENTER * g for i, g in zip(unpacked_image(), gram)]
    image = jnp.concatenate(image, 0)[:, :64]
    one = dot(dot(narrow, image, NN), inverse, NT)
    two = dot(dot(inverse, image, NT), narrow, NT)
    projected[...] = 0.5 * (one + two)

    for side in range(2):

        @pl.when(has[1 - side])
        def _():
            pot_copy(side).wait_send()
            for g in range(2):
                far_copy(g, side).wait_send()
                for s in range(DEGREE):
                    for part in range(PARTS):
                        halo_copy(s, g, side, part).wait_send()

    for g in range(2):
        for part in range(PARTS):
            sibling_copy(g, part).wait_send()
    for m, f in SUMS:
        for d in range(1, phases[f][0]):
            reduce_copy(m, f, d).wait_send()
    out.wait()


def eliminated(rows, subs):
    def spread(value):
        return jnp.broadcast_to(value, (8, 128))

    rows = list(rows)
    for r in range(4):
        lane = 16 * r
        column = {
            q: [spread(rows[q][:, lane + b : lane + b + 1]) for b in range(8)] for q in range(r, 4)
        }
        block = [[spread(column[r][b][a : a + 1]) for b in range(a + 1)] for a in range(8)]
        pivot = [spread(rows[r][a : a + 1]) for a in range(8)]
        factor = {q: [None] * 8 for q in range(r + 1, 4)}
        for k in range(8):
            reciprocal = 1.0 / block[k][k]
            for a in range(k + 1, 8):
                ratio = block[a][k] * reciprocal
                for b in range(k + 1, a + 1):
                    block[a][b] = block[a][b] - ratio * block[b][k]
                pivot[a] = pivot[a] - ratio * pivot[k]
            for q in range(r + 1, 4):
                factor[q][k] = column[q][k] * reciprocal
                for b in range(k + 1, 8):
                    column[q][b] = column[q][b] - factor[q][k] * block[b][k]
        for q in range(r + 1, 4):
            for k in range(8):
                rows[q] = rows[q] - factor[q][k] * pivot[k]
        done = pivot[0] * lax.rsqrt(block[0][0])
        for k in range(1, 8):
            done = jnp.where(subs == k, pivot[k] * lax.rsqrt(block[k][k]), done)
        rows[r] = done
    return rows


def shards(trial_block, potential):
    rings = RINGS[lax.axis_size("dom")]
    most = max(2 * rings[2], rings[0] // 2 * rings[1])
    f32, dma = jnp.float32, pltpu.SemaphoreType.DMA
    orbitals, projected = pl.pallas_call(
        functools.partial(kernel, rings),
        out_shape=(
            jax.ShapeDtypeStruct((1024, 128), f32),
            jax.ShapeDtypeStruct((32, 32), f32),
        ),
        in_specs=[pl.BlockSpec(memory_space=pl.ANY)] * 2,
        out_specs=(
            pl.BlockSpec(memory_space=pl.ANY),
            pl.BlockSpec(memory_space=pltpu.VMEM),
        ),
        scratch_shapes=[
            pltpu.VMEM((1024, 128), f32),
            pltpu.VMEM((8, 8, 128), f32),
            pltpu.VMEM((2, 2, 8, 128), f32),
            pltpu.VMEM((8, 8, 8, 128), f32),
            pltpu.VMEM((2, 2, 8, 8, 128), f32),
            pltpu.VMEM((DEGREE + 2, 2, 16, 8, 8, 128), f32),
            pltpu.VMEM((DEGREE, 2, 2, 4, 8, 8, 128), f32),
            pltpu.VMEM((2, 2, 2, 8, 8, 128), f32),
            pltpu.VMEM((2, 8, 8, 8, 128), f32),
            pltpu.VMEM((32, 64, 256), jnp.bfloat16),
            pltpu.VMEM((32, 32, 256), jnp.bfloat16),
            pltpu.VMEM((64, 128), f32),
            pltpu.VMEM((2, 3, most, 8, 128), f32),
            dma((3,)),
            dma((DEGREE, 2, 2, PARTS)),
            dma((DEGREE, 2, 2, PARTS)),
            dma((3, 2)),
            dma((3, 2)),
            dma((2, PARTS)),
            dma((2, PARTS)),
            dma((2, 3, most)),
            dma((2, 3, most)),
        ],
        compiler_params=pltpu.CompilerParams(
            collective_id=0, has_side_effects=True, vmem_limit_bytes=60 * 1024 * 1024
        ),
        cost_estimate=pl.CostEstimate(
            flops=200_000_000, bytes_accessed=1_100_000, transcendentals=0
        ),
    )(trial_block.reshape(1024, 128), potential)
    return orbitals.reshape(trial_block.shape), projected


def solution(mesh):
    return jax.shard_map(
        shards,
        mesh=mesh,
        in_specs=(P("band", "dom", None, None), P("dom", None, None)),
        out_specs=(P("band", "dom", None, None), P()),
        check_vma=False,
    )
```

```python
import functools

import jax
import jax.numpy as jnp
from jax import lax
from jax.experimental import pallas as pl
from jax.experimental.pallas import tpu as pltpu
from jax.sharding import PartitionSpec as P

COEFFS = (-205.0 / 72.0, 8.0 / 5.0, -1.0 / 5.0, 8.0 / 315.0, -1.0 / 560.0)
CENTER = 5.75
HALF_WIDTH = 5.25
DEGREE = 4

PAIR = tuple(-0.5 * c / HALF_WIDTH for c in COEFFS)
DIAG = -1.5 * COEFFS[0] - CENTER

MESH = pl.DeviceIdType.MESH
NT = (((1,), (1,)), ((), ()))
NN = (((1,), (0,)), ((), ()))
PARTS = 2
YS = 8 // PARTS
SHIFT = (0, 8, 64, 72)
RINGS = {256: (4, 8, 8), 8: (2, 2, 2)}


def far_first(count):
    return sorted(range(1, count), key=lambda d: -min(d, count - d))


def kernel(
    rings,
    trial,
    potential,
    orbitals,
    projected,
    nat,
    pot,
    pot_far,
    weight,
    weight_far,
    field,
    halo,
    far,
    other,
    split,
    usplit,
    border,
    weighted,
    tile,
    slots,
    thin,
    in_sem,
    halo_send,
    halo_recv,
    far_send,
    far_recv,
    sib_send,
    sib_recv,
    red_send,
    red_recv,
):
    nx, nz, ny = rings
    doms = nx * nz * ny
    cells = doms * 8 * 8 * 128
    dom = lax.axis_index("dom")
    band = lax.axis_index("band")
    py = lax.rem(dom, ny)
    pz = lax.rem(lax.div(dom, ny), nz)
    px = lax.div(dom, ny * nz)
    left = lax.rem(dom + doms - 1, doms)
    right = lax.rem(dom + 1, doms)

    def at(x, z, y):
        return (x * nz + z) * ny + y

    pairs = nx // 2
    half = lax.div(px, 2)

    def member_yx(p):
        x = 2 * half + lax.rem(p, 2)
        return {"dom": at(x, pz, lax.div(p, 2)), "band": band}

    def member_core(p):
        return {**member_yx(lax.div(p, 2)), "band": lax.rem(p, 2)}

    def member_zx(p):
        x = jnp.where(lax.rem(p, pairs) == half, px, nx - 1 - px)
        return {"dom": at(x, lax.div(p, pairs), py), "band": band}

    place_yx = 2 * py + lax.rem(px, 2)
    along_z = (pairs * nz, pairs * pz + half, member_zx)
    sums = (
        (2 * ny, place_yx, member_yx, slots.at[0]),
        (*along_z, slots.at[1]),
        (4 * ny, 2 * place_yx + band, member_core, thin),
        (*along_z, slots.at[2]),
    )

    loads = [
        pltpu.make_async_copy(potential, pot, in_sem.at[2]),
        pltpu.make_async_copy(trial.at[pl.ds(0, 512)], nat.at[pl.ds(0, 512)], in_sem.at[0]),
        pltpu.make_async_copy(trial.at[pl.ds(512, 512)], nat.at[pl.ds(512, 512)], in_sem.at[1]),
    ]
    for load in loads:
        load.start()

    barrier = pltpu.get_barrier_semaphore()
    greeted = 0
    for count, place, member, _ in sums[1:3]:
        for d in far_first(count):
            pl.semaphore_signal(
                barrier, inc=1, device_id=member(lax.rem(place + d, count)), device_id_type=MESH
            )
            greeted += 1
    for neighbour in (left, right):
        pl.semaphore_signal(
            barrier, inc=1, device_id={"dom": neighbour, "band": band}, device_id_type=MESH
        )
        greeted += 1

    zeros = jnp.zeros((4, 8, 8, 128), jnp.float32)

    def clear(i, carry):
        s, g = lax.div(i, 2), lax.rem(i, 2)
        field[s, g, pl.ds(0, 4)] = zeros
        field[s, g, pl.ds(12, 4)] = zeros
        return carry

    def spread_weight(target, rows):
        rows = (rows + DIAG) * (1.0 / HALF_WIDTH)
        for y in range(8):
            target[y] = jnp.broadcast_to(rows[y : y + 1], (8, 128))

    def set_weight(x, carry):
        spread_weight(weight.at[x], pot[x])
        return carry

    def relayout(g):
        def body(x, carry):
            for y in range(8):
                field[0, g, 4 + x, y] = nat[pl.ds(g * 512 + x * 8 + y, 8, stride=64), :]
            return carry

        lax.fori_loop(0, 8, body, 0)

    has = (dom > 0, dom < doms - 1)

    def to_neighbour(side, src, dst, send_sem, recv_sem):
        return pltpu.make_async_remote_copy(
            src_ref=src,
            dst_ref=dst,
            send_sem=send_sem,
            recv_sem=recv_sem,
            device_id={"dom": right if side == 0 else left, "band": band},
            device_id_type=MESH,
        )

    def halo_copy(s, g, side, part):
        ys = pl.ds(part * YS, YS)
        return to_neighbour(
            side,
            field.at[s, g, pl.ds(8 if side == 0 else 4, 4), ys],
            halo.at[s, g, side, :, ys],
            halo_send.at[s, g, side, part],
            halo_recv.at[s, g, side, part],
        )

    def far_copy(g, side):
        return to_neighbour(
            side,
            field.at[last, g, pl.ds(6 if side == 0 else 8, 2)],
            far.at[g, side],
            far_send.at[g, side],
            far_recv.at[g, side],
        )

    def pot_copy(side):
        return to_neighbour(
            side,
            pot.at[pl.ds(6 if side == 0 else 0, 2)],
            pot_far.at[side],
            far_send.at[2, side],
            far_recv.at[2, side],
        )

    def send(side, copy):
        @pl.when(has[1 - side])
        def _():
            copy.start()

    lane = lax.broadcasted_iota(jnp.int32, (8, 8, 128), 2)

    def shifted_y(c, k):
        empty = jnp.zeros((k, 8, 128), jnp.float32)
        return jnp.concatenate([c[k:], empty], 0) + jnp.concatenate([empty, c[: 8 - k]], 0)

    def shifted_z(c, k):
        below = jnp.where(lane >= k, pltpu.roll(c, k, 2), 0.0)
        return below + jnp.where(lane < 128 - k, pltpu.roll(c, 128 - k, 2), 0.0)

    def local_part(s, g):
        def body(x, carry):
            c = field[s, g, 4 + x]
            total = weight[x] * c
            for k in range(1, 5):
                pairs = field[s, g, 4 + x + k] + field[s, g, 4 + x - k]
                pairs = pairs + shifted_y(c, k) + shifted_z(c, k)
                total = total + PAIR[k] * pairs
            if 1 <= s < DEGREE:
                total = 2.0 * total - field[s - 1, g, 4 + x]
            field[s + 1, g, 4 + x] = total
            return carry

        lax.fori_loop(0, 8, body, 0)

    def halo_part(s, g, side, part):
        twice = 1.0 if s == 0 else 2.0
        ys = pl.ds(part * YS, YS)
        layers = {n: halo[s, g, side, 4 - n if side == 0 else n - 1, ys] for n in range(1, 5)}
        for x in range(4):
            mine = 4 + x if side == 0 else 11 - x
            total = field[s + 1, g, mine, ys]
            for n in range(1, 5 - x):
                total = total + (twice * PAIR[x + n]) * layers[n]
            field[s + 1, g, mine, ys] = total

    def border_part(g, side):
        def cell(n):
            if n > 4:
                return far[g, side, 6 - n if side == 0 else n - 5]
            if n > 0:
                return halo[last, g, side, 4 - n if side == 0 else n - 1]
            return field[last, g, 4 - n if side == 0 else 11 + n]

        for n in (1, 2):
            c = cell(n)
            total = weight_far[side, 2 - n if side == 0 else n - 1] * c
            for k in range(1, 5):
                near = cell(n + k) + cell(n - k) + shifted_y(c, k) + shifted_z(c, k)
                total = total + PAIR[k] * near
            total = 2.0 * total - halo[last - 1, g, side, 4 - n if side == 0 else n - 1]
            split_layer(side, n, g, total)

    def sibling_copy(g, part):
        ys = pl.ds(part * YS, YS)
        return pltpu.make_async_remote_copy(
            src_ref=field.at[DEGREE, g, pl.ds(4, 8), ys],
            dst_ref=other.at[g, :, ys],
            send_sem=sib_send.at[g, part],
            recv_sem=sib_recv.at[g, part],
            device_id={"dom": dom, "band": 1 - band},
            device_id_type=MESH,
        )

    def sum_copy(f, d):
        count, place, member, into = sums[f]
        return pltpu.make_async_remote_copy(
            src_ref=into.at[place],
            dst_ref=into.at[place],
            send_sem=red_send.at[f, d],
            recv_sem=red_recv.at[f, place],
            device_id=member(lax.rem(place + d, count)),
            device_id_type=MESH,
        )

    def sum_start(f, value):
        count, place, _, into = sums[f]
        into[place] = value
        for d in far_first(count):
            sum_copy(f, d).start()

    def summed(f):
        count, place, member, into = sums[f]
        for d in range(1, count):
            source = lax.rem(place + d, count)
            pltpu.make_async_remote_copy(
                src_ref=into.at[source],
                dst_ref=into.at[source],
                send_sem=red_send.at[f, d],
                recv_sem=red_recv.at[f, source],
                device_id=member(source),
                device_id_type=MESH,
            ).wait_recv()
        step = 2 if f == 2 else 1
        totals = []
        for first in range(step):
            total = into[first]
            for p in range(first + step, count, step):
                total = total + into[p]
            totals.append(total)
        return jnp.concatenate(totals, 0)

    def split_rows(value):
        high = value.astype(jnp.bfloat16).astype(jnp.float32)
        return jnp.concatenate([high, value - high], 0).astype(jnp.bfloat16)

    def lanes_at(x, y):
        return pl.ds(128 * (8 * YS * (y // YS) + YS * x + y % YS), 128)

    def split_into(target, first, ys, read):
        for x in range(8):
            for y in ys:
                target[pl.ds(first, 16), lanes_at(x, y)] = split_rows(read(x, y))

    own_rows = pl.multiple_of(band * 32, 32)
    other_rows = pl.multiple_of(32 - band * 32, 32)

    def of_part(part):
        return range(part * YS, (part + 1) * YS)

    def split_own(g, part):
        first = own_rows + 16 * g
        split_into(split, first, of_part(part), lambda x, y: field[DEGREE, g, 4 + x, y])

    def split_other(g, part):
        split_into(split, other_rows + 16 * g, of_part(part), lambda x, y: other[g, x, y])

    def product(left, right):
        return lax.dot_general(left, right, NT, preferred_element_type=jnp.float32)

    def gram_part(part, total):
        rows = split[:, pl.ds(part * YS * 1024, YS * 1024)]
        return total + product(rows, rows)

    def split_layer(side, n, g, value):
        for y in range(8):
            at_y = pl.ds(128 * (16 * side + 8 * n - 8 + y), 128)
            border[pl.ds(16 * g, 16), at_y] = split_rows(value[y])

    def weigh(first, read):
        for side in range(2):
            for n in (1, 2):
                for y in range(8):
                    total = None
                    for x in range(0 if side == 0 else 2, 5 - n):
                        value = (2.0 * PAIR[x + n]) * read(x if side == 0 else 7 - x, y)
                        total = value if total is None else total + value
                    at_y = pl.ds(128 * (16 * side + 8 * n - 8 + y), 128)
                    weighted[pl.ds(first, 16), at_y] = split_rows(total)

    def weigh_own(g):
        weigh(own_rows + 16 * g, lambda x, y: field[DEGREE, g, 4 + x, y])

    def weigh_other(g):
        weigh(other_rows + 16 * g, lambda x, y: other[g, x, y])

    def image_rows(g):
        local_part(DEGREE, g)
        split_into(usplit, 16 * g, range(8), lambda x, y: field[DEGREE + 1, g, 4 + x, y])
        weigh_own(g)

    lanes = lax.broadcasted_iota(jnp.int32, (8, 128), 1)
    subs = lax.broadcasted_iota(jnp.int32, (8, 128), 0)
    used = (lanes < 64) & (lax.rem(lanes, 16) < 8)

    def folded(value):
        return value + pltpu.roll(value, 120, 1)

    def packed_gram(total):
        tile[:, pl.ds(0, 64)] = total
        value = jnp.zeros((8, 128), jnp.float32)
        for q in range(4):
            row = folded(tile[pl.ds(16 * q, 8)] + tile[pl.ds(16 * q + 8, 8)])
            row = jnp.where(used, row, 0.0)
            value = value + (row if q == 0 else pltpu.roll(row, SHIFT[q], 1))
        return value

    def unpacked_gram(value):
        rows = [value] + [pltpu.roll(value, 128 - SHIFT[q], 1) for q in range(1, 4)]
        return [jnp.where(used, row, 0.0) for row in rows]

    def packed_image(total):
        tile[pl.ds(0, 8), pl.ds(0, 64)] = total[:8] + total[8:16]
        tile[pl.ds(8, 8), pl.ds(0, 64)] = total[16:24] + total[24:]
        one, two = [jnp.where(used, folded(tile[pl.ds(8 * g, 8)]), 0.0) for g in range(2)]
        both = one + pltpu.roll(two, 8, 1)
        return (both + pltpu.roll(pltpu.roll(both, 64, 1), 4, 0))[:4]

    def unpacked_image(value):
        moved = pltpu.roll(value, 64, 1)
        one = jnp.where(subs < 4, value, pltpu.roll(moved, 4, 0))
        two = jnp.where(subs < 4, pltpu.roll(value, 4, 0), moved)
        rows = [one, pltpu.roll(one, 120, 1), two, pltpu.roll(two, 120, 1)]
        return [jnp.where(used, row, 0.0) for row in rows]

    last = DEGREE - 1

    for g in range(2):
        loads[1 + g].wait()
        relayout(g)
        if g == 0:
            pl.semaphore_wait(barrier, greeted)
        for part in range(PARTS):
            for side in range(2):
                send(side, halo_copy(0, g, side, part))
    loads[0].wait()
    for side in range(2):
        send(side, pot_copy(side))
    lax.fori_loop(0, 2 * (DEGREE + 1), clear, 0)
    tile[...] = jnp.zeros((64, 128), jnp.float32)
    lax.fori_loop(0, 8, set_weight, 0)
    for g in range(2):
        local_part(0, g)

    for s in range(last):
        for g in range(2):

            def exchange(part, carry):
                for side in range(2):

                    @pl.when(has[side])
                    def _():
                        halo_copy(s, g, side, part).wait_recv()
                        halo_part(s, g, side, part)
                        halo_copy(s + 1, g, 1 - side, part).start()

                return carry

            lax.fori_loop(0, PARTS, exchange, 0)
            local_part(s + 1, g)
    for g in range(2):
        for side in range(2):
            send(side, far_copy(g, side))

    for side in range(2):

        @pl.when(has[side])
        def _():
            pot_copy(side).wait_recv()
            for n in range(2):
                spread_weight(weight_far.at[side, n], pot_far[side, n])

    gram = jnp.zeros((64, 64), jnp.float32)
    for g in range(2):
        for part in range(PARTS):
            for side in range(2):

                @pl.when(has[side])
                def _():
                    halo_copy(last, g, side, part).wait_recv()
                    halo_part(last, g, side, part)

            sibling_copy(g, part).start()
            split_own(g, part)
            if part > 0:
                sibling_copy(g, part - 1).wait_recv()
                split_other(g, part - 1)
                if g == 1:
                    gram = gram_part(part - 1, gram)
        image_rows(g)
        sibling_copy(g, PARTS - 1).wait_recv()
        split_other(g, PARTS - 1)
        if g == 0:
            weigh_other(0)
    sum_start(0, packed_gram(gram_part(PARTS - 1, gram)))

    image = product(usplit[...], split[...])
    weigh_other(1)
    for side in range(2):

        @pl.when(has[side])
        def _():
            for g in range(2):
                far_copy(g, side).wait_recv()
                border_part(g, side)

        @pl.when(jnp.logical_not(has[side]))
        def _():
            border[:, pl.ds(2048 * side, 2048)] = jnp.zeros((32, 2048), jnp.bfloat16)

    sum_start(2, packed_image(image + product(border[...], weighted[...])))
    sum_start(1, summed(0))
    sum_start(3, summed(2))

    gram = [row * (1.0 / cells) for row in unpacked_gram(summed(1))]
    rows = [jnp.where(lanes == subs + (64 + 16 * q), 1.0, gram[q]) for q in range(4)]
    inverse = eliminated(rows, subs)
    inverse = [jnp.where(used, pltpu.roll(row, 64, 1), 0.0) for row in inverse]

    own = [jnp.where(band == 0, inverse[q], inverse[2 + q]) for q in range(2)]
    own = split_rows(jnp.concatenate([v + pltpu.roll(v, 8, 1) for v in own], 0))[:, :64]

    for part in range(PARTS):
        for x in range(8):
            at_x = pl.ds(128 * YS * (8 * part + x), 128 * YS)
            value = lax.dot_general(own, split[:, at_x], NN, preferred_element_type=jnp.float32)
            value = value[:16] + value[16:]
            for y in range(YS):
                row = x * 8 + part * YS + y
                nat[pl.ds(row, 16, stride=64), :] = value[:, 128 * y : 128 * y + 128]
    out = pltpu.make_async_copy(nat, orbitals, in_sem.at[0])
    out.start()

    dot = functools.partial(
        lax.dot_general, precision=lax.Precision.HIGHEST, preferred_element_type=jnp.float32
    )
    inverse = jnp.concatenate(inverse, 0)[:, :64]
    column = lax.broadcasted_iota(jnp.int32, (64, 32), 1)
    spread = lax.broadcasted_iota(jnp.int32, (64, 32), 0)
    spread = spread == 16 * lax.div(column, 8) + lax.rem(column, 8)
    narrow = dot(inverse, jnp.where(spread, 1.0, 0.0), NN)
    image = [(HALF_WIDTH / cells) * i + CENTER * g for i, g in zip(unpacked_image(summed(3)), gram)]
    image = jnp.concatenate(image, 0)[:, :64]
    one = dot(dot(narrow, image, NN), inverse, NT)
    two = dot(dot(inverse, image, NT), narrow, NT)
    projected[...] = 0.5 * (one + two)

    for side in range(2):

        @pl.when(has[1 - side])
        def _():
            pot_copy(side).wait_send()
            for g in range(2):
                far_copy(g, side).wait_send()
                for s in range(DEGREE):
                    for part in range(PARTS):
                        halo_copy(s, g, side, part).wait_send()

    for g in range(2):
        for part in range(PARTS):
            sibling_copy(g, part).wait_send()
    for f in range(4):
        for d in range(1, sums[f][0]):
            sum_copy(f, d).wait_send()
    out.wait()


def eliminated(rows, subs):
    def spread(value):
        return jnp.broadcast_to(value, (8, 128))

    rows = list(rows)
    for r in range(4):
        lane = 16 * r
        column = {
            q: [spread(rows[q][:, lane + b : lane + b + 1]) for b in range(8)] for q in range(r, 4)
        }
        block = [[spread(column[r][b][a : a + 1]) for b in range(a + 1)] for a in range(8)]
        pivot = [spread(rows[r][a : a + 1]) for a in range(8)]
        factor = {q: [None] * 8 for q in range(r + 1, 4)}
        for k in range(8):
            reciprocal = 1.0 / block[k][k]
            for a in range(k + 1, 8):
                ratio = block[a][k] * reciprocal
                for b in range(k + 1, a + 1):
                    block[a][b] = block[a][b] - ratio * block[b][k]
                pivot[a] = pivot[a] - ratio * pivot[k]
            for q in range(r + 1, 4):
                factor[q][k] = column[q][k] * reciprocal
                for b in range(k + 1, 8):
                    column[q][b] = column[q][b] - factor[q][k] * block[b][k]
        for q in range(r + 1, 4):
            for k in range(8):
                rows[q] = rows[q] - factor[q][k] * pivot[k]
        done = pivot[0] * lax.rsqrt(block[0][0])
        for k in range(1, 8):
            done = jnp.where(subs == k, pivot[k] * lax.rsqrt(block[k][k]), done)
        rows[r] = done
    return rows


def shards(trial_block, potential):
    rings = RINGS[lax.axis_size("dom")]
    most = max(2 * rings[2], rings[0] // 2 * rings[1])
    f32, dma = jnp.float32, pltpu.SemaphoreType.DMA
    orbitals, projected = pl.pallas_call(
        functools.partial(kernel, rings),
        out_shape=(
            jax.ShapeDtypeStruct((1024, 128), f32),
            jax.ShapeDtypeStruct((32, 32), f32),
        ),
        in_specs=[pl.BlockSpec(memory_space=pl.ANY)] * 2,
        out_specs=(
            pl.BlockSpec(memory_space=pl.ANY),
            pl.BlockSpec(memory_space=pltpu.VMEM),
        ),
        scratch_shapes=[
            pltpu.VMEM((1024, 128), f32),
            pltpu.VMEM((8, 8, 128), f32),
            pltpu.VMEM((2, 2, 8, 128), f32),
            pltpu.VMEM((8, 8, 8, 128), f32),
            pltpu.VMEM((2, 2, 8, 8, 128), f32),
            pltpu.VMEM((DEGREE + 2, 2, 16, 8, 8, 128), f32),
            pltpu.VMEM((DEGREE, 2, 2, 4, 8, 8, 128), f32),
            pltpu.VMEM((2, 2, 2, 8, 8, 128), f32),
            pltpu.VMEM((2, 8, 8, 8, 128), f32),
            pltpu.VMEM((64, 8192), jnp.bfloat16),
            pltpu.VMEM((32, 8192), jnp.bfloat16),
            pltpu.VMEM((32, 4096), jnp.bfloat16),
            pltpu.VMEM((64, 4096), jnp.bfloat16),
            pltpu.VMEM((64, 128), f32),
            pltpu.VMEM((3, most, 8, 128), f32),
            pltpu.VMEM((4 * rings[2], 4, 128), f32),
            dma((3,)),
            dma((DEGREE, 2, 2, PARTS)),
            dma((DEGREE, 2, 2, PARTS)),
            dma((3, 2)),
            dma((3, 2)),
            dma((2, PARTS)),
            dma((2, PARTS)),
            dma((4, 4 * rings[2])),
            dma((4, 4 * rings[2])),
        ],
        compiler_params=pltpu.CompilerParams(
            collective_id=0, has_side_effects=True, vmem_limit_bytes=60 * 1024 * 1024
        ),
        cost_estimate=pl.CostEstimate(
            flops=200_000_000, bytes_accessed=1_100_000, transcendentals=0
        ),
    )(trial_block.reshape(1024, 128), potential)
    return orbitals.reshape(trial_block.shape), projected


def solution(mesh):
    return jax.shard_map(
        shards,
        mesh=mesh,
        in_specs=(P("band", "dom", None, None), P("dom", None, None)),
        out_specs=(P("band", "dom", None, None), P()),
        check_vma=False,
    )
```

```python
import functools

import jax
import jax.numpy as jnp
from jax import lax
from jax.experimental import pallas as pl
from jax.experimental.pallas import tpu as pltpu
from jax.sharding import PartitionSpec as P

COEFFS = (-205.0 / 72.0, 8.0 / 5.0, -1.0 / 5.0, 8.0 / 315.0, -1.0 / 560.0)
CENTER = 5.75
HALF_WIDTH = 5.25
DEGREE = 4

PAIR = tuple(-0.5 * c / HALF_WIDTH for c in COEFFS)
DIAG = -1.5 * COEFFS[0] - CENTER

MESH = pl.DeviceIdType.MESH
NT = (((1,), (1,)), ((), ()))
NN = (((1,), (0,)), ((), ()))
PARTS = 2
YS = 8 // PARTS
SHIFT = (0, 8, 64, 72)
RINGS = {256: (4, 8, 8), 8: (2, 2, 2)}


def far_first(count):
    return sorted(range(1, count), key=lambda d: -min(d, count - d))


def kernel(
    rings,
    trial,
    potential,
    orbitals,
    projected,
    nat,
    pot,
    pot_far,
    weight,
    weight_far,
    field,
    halo,
    far,
    other,
    split,
    usplit,
    border,
    weighted,
    tile,
    slots,
    thin,
    in_sem,
    halo_send,
    halo_recv,
    far_send,
    far_recv,
    sib_send,
    sib_recv,
    red_send,
    red_recv,
    known,
):
    nx, nz, ny = rings
    doms = nx * nz * ny
    cells = doms * 8 * 8 * 128
    dom = lax.axis_index("dom")
    band = lax.axis_index("band")
    py = lax.rem(dom, ny)
    pz = lax.rem(lax.div(dom, ny), nz)
    px = lax.div(dom, ny * nz)
    left = lax.rem(dom + doms - 1, doms)
    right = lax.rem(dom + 1, doms)

    def at(x, z, y):
        return (x * nz + z) * ny + y

    pairs = nx // 2
    half = lax.div(px, 2)

    def member_yx(p):
        x = 2 * half + lax.rem(p, 2)
        return {"dom": at(x, pz, lax.div(p, 2)), "band": band}

    def member_core(p):
        return {**member_yx(lax.div(p, 2)), "band": lax.rem(p, 2)}

    def member_zx(p):
        x = jnp.where(lax.rem(p, pairs) == half, px, nx - 1 - px)
        return {"dom": at(x, lax.div(p, pairs), py), "band": band}

    place_yx = 2 * py + lax.rem(px, 2)
    along_z = (pairs * nz, pairs * pz + half, member_zx)
    sums = (
        (2 * ny, place_yx, member_yx, slots.at[0]),
        (*along_z, slots.at[1]),
        (4 * ny, 2 * place_yx + band, member_core, thin),
        (*along_z, slots.at[2]),
    )

    loads = [
        pltpu.make_async_copy(potential, pot, in_sem.at[2]),
        pltpu.make_async_copy(trial.at[pl.ds(0, 512)], nat.at[pl.ds(0, 512)], in_sem.at[0]),
        pltpu.make_async_copy(trial.at[pl.ds(512, 512)], nat.at[pl.ds(512, 512)], in_sem.at[1]),
    ]
    for load in loads:
        load.start()

    def along(axis, steps):
        where = [px, pz, py]
        size = rings[axis]
        where[axis] = lax.rem(where[axis] + steps + size, size)
        return {"dom": at(*where), "band": band}

    one_hop = [along(axis, way) for axis in range(3) for way in (1, -1)]
    two_hops = [
        along(axis, way)
        for axis in (1, 2)
        for way in (2, -2)
        if rings[axis] > 2
    ]
    sibling = {"dom": dom, "band": 1 - band}

    barrier = pltpu.get_barrier_semaphore()
    nearest = one_hop + [{"dom": d, "band": band} for d in (left, right)] + [sibling]
    for device in nearest:
        pl.semaphore_signal(barrier, inc=1, device_id=device, device_id_type=MESH)
    rounds = (one_hop, two_hops, two_hops, [sibling])

    def tell(r):
        for i, device in enumerate(rounds[r]):
            pl.semaphore_signal(
                known.at[r, i], inc=1, device_id=device, device_id_type=MESH
            )

    def hear(r):
        for i in range(len(rounds[r])):
            pl.semaphore_wait(known.at[r, i], 1)

    zeros = jnp.zeros((4, 8, 8, 128), jnp.float32)

    def clear(i, carry):
        s, g = lax.div(i, 2), lax.rem(i, 2)
        field[s, g, pl.ds(0, 4)] = zeros
        field[s, g, pl.ds(12, 4)] = zeros
        return carry

    def spread_weight(target, rows):
        rows = (rows + DIAG) * (1.0 / HALF_WIDTH)
        for y in range(8):
            target[y] = jnp.broadcast_to(rows[y : y + 1], (8, 128))

    def set_weight(x, carry):
        spread_weight(weight.at[x], pot[x])
        return carry

    def relayout(g):
        def body(x, carry):
            for y in range(8):
                field[0, g, 4 + x, y] = nat[pl.ds(g * 512 + x * 8 + y, 8, stride=64), :]
            return carry

        lax.fori_loop(0, 8, body, 0)

    has = (dom > 0, dom < doms - 1)

    def to_neighbour(side, src, dst, send_sem, recv_sem):
        return pltpu.make_async_remote_copy(
            src_ref=src,
            dst_ref=dst,
            send_sem=send_sem,
            recv_sem=recv_sem,
            device_id={"dom": right if side == 0 else left, "band": band},
            device_id_type=MESH,
        )

    def halo_copy(s, g, side, part):
        ys = pl.ds(part * YS, YS)
        return to_neighbour(
            side,
            field.at[s, g, pl.ds(8 if side == 0 else 4, 4), ys],
            halo.at[s, g, side, :, ys],
            halo_send.at[s, g, side, part],
            halo_recv.at[s, g, side, part],
        )

    def far_copy(g, side):
        return to_neighbour(
            side,
            field.at[last, g, pl.ds(6 if side == 0 else 8, 2)],
            far.at[g, side],
            far_send.at[g, side],
            far_recv.at[g, side],
        )

    def pot_copy(side):
        return to_neighbour(
            side,
            pot.at[pl.ds(6 if side == 0 else 0, 2)],
            pot_far.at[side],
            far_send.at[2, side],
            far_recv.at[2, side],
        )

    def send(side, copy):
        @pl.when(has[1 - side])
        def _():
            copy.start()

    lane = lax.broadcasted_iota(jnp.int32, (8, 8, 128), 2)

    def shifted_y(c, k):
        empty = jnp.zeros((k, 8, 128), jnp.float32)
        return jnp.concatenate([c[k:], empty], 0) + jnp.concatenate([empty, c[: 8 - k]], 0)

    def shifted_z(c, k):
        below = jnp.where(lane >= k, pltpu.roll(c, k, 2), 0.0)
        return below + jnp.where(lane < 128 - k, pltpu.roll(c, 128 - k, 2), 0.0)

    def local_part(s, g):
        def body(x, carry):
            c = field[s, g, 4 + x]
            total = weight[x] * c
            for k in range(1, 5):
                pairs = field[s, g, 4 + x + k] + field[s, g, 4 + x - k]
                pairs = pairs + shifted_y(c, k) + shifted_z(c, k)
                total = total + PAIR[k] * pairs
            if 1 <= s < DEGREE:
                total = 2.0 * total - field[s - 1, g, 4 + x]
            field[s + 1, g, 4 + x] = total
            return carry

        lax.fori_loop(0, 8, body, 0)

    def halo_part(s, g, side, part):
        twice = 1.0 if s == 0 else 2.0
        ys = pl.ds(part * YS, YS)
        layers = {n: halo[s, g, side, 4 - n if side == 0 else n - 1, ys] for n in range(1, 5)}
        for x in range(4):
            mine = 4 + x if side == 0 else 11 - x
            total = field[s + 1, g, mine, ys]
            for n in range(1, 5 - x):
                total = total + (twice * PAIR[x + n]) * layers[n]
            field[s + 1, g, mine, ys] = total

    def border_part(g, side):
        def cell(n):
            if n > 4:
                return far[g, side, 6 - n if side == 0 else n - 5]
            if n > 0:
                return halo[last, g, side, 4 - n if side == 0 else n - 1]
            return field[last, g, 4 - n if side == 0 else 11 + n]

        for n in (1, 2):
            c = cell(n)
            total = weight_far[side, 2 - n if side == 0 else n - 1] * c
            for k in range(1, 5):
                near = cell(n + k) + cell(n - k) + shifted_y(c, k) + shifted_z(c, k)
                total = total + PAIR[k] * near
            total = 2.0 * total - halo[last - 1, g, side, 4 - n if side == 0 else n - 1]
            split_layer(side, n, g, total)

    def sibling_copy(g, part):
        ys = pl.ds(part * YS, YS)
        return pltpu.make_async_remote_copy(
            src_ref=field.at[DEGREE, g, pl.ds(4, 8), ys],
            dst_ref=other.at[g, :, ys],
            send_sem=sib_send.at[g, part],
            recv_sem=sib_recv.at[g, part],
            device_id={"dom": dom, "band": 1 - band},
            device_id_type=MESH,
        )

    def sum_copy(f, d):
        count, place, member, into = sums[f]
        return pltpu.make_async_remote_copy(
            src_ref=into.at[place],
            dst_ref=into.at[place],
            send_sem=red_send.at[f, d],
            recv_sem=red_recv.at[f, place],
            device_id=member(lax.rem(place + d, count)),
            device_id_type=MESH,
        )

    def sum_start(f, value):
        count, place, _, into = sums[f]
        into[place] = value
        for d in far_first(count):
            sum_copy(f, d).start()

    def summed(f):
        count, place, member, into = sums[f]
        for d in range(1, count):
            source = lax.rem(place + d, count)
            pltpu.make_async_remote_copy(
                src_ref=into.at[source],
                dst_ref=into.at[source],
                send_sem=red_send.at[f, d],
                recv_sem=red_recv.at[f, source],
                device_id=member(source),
                device_id_type=MESH,
            ).wait_recv()
        step = 2 if f == 2 else 1
        totals = []
        for first in range(step):
            total = into[first]
            for p in range(first + step, count, step):
                total = total + into[p]
            totals.append(total)
        return jnp.concatenate(totals, 0)

    def split_rows(value):
        high = value.astype(jnp.bfloat16).astype(jnp.float32)
        return jnp.concatenate([high, value - high], 0).astype(jnp.bfloat16)

    def lanes_at(x, y):
        return pl.ds(128 * (8 * YS * (y // YS) + YS * x + y % YS), 128)

    def split_into(target, first, ys, read):
        for x in range(8):
            for y in ys:
                target[pl.ds(first, 16), lanes_at(x, y)] = split_rows(read(x, y))

    own_rows = pl.multiple_of(band * 32, 32)
    other_rows = pl.multiple_of(32 - band * 32, 32)

    def of_part(part):
        return range(part * YS, (part + 1) * YS)

    def split_own(g, part):
        first = own_rows + 16 * g
        split_into(split, first, of_part(part), lambda x, y: field[DEGREE, g, 4 + x, y])

    def split_other(g, part):
        split_into(split, other_rows + 16 * g, of_part(part), lambda x, y: other[g, x, y])

    def product(left, right):
        return lax.dot_general(left, right, NT, preferred_element_type=jnp.float32)

    def gram_part(part, total):
        rows = split[:, pl.ds(part * YS * 1024, YS * 1024)]
        return total + product(rows, rows)

    def split_layer(side, n, g, value):
        for y in range(8):
            at_y = pl.ds(128 * (16 * side + 8 * n - 8 + y), 128)
            border[pl.ds(16 * g, 16), at_y] = split_rows(value[y])

    def weigh(first, read):
        for side in range(2):
            for n in (1, 2):
                for y in range(8):
                    total = None
                    for x in range(0 if side == 0 else 2, 5 - n):
                        value = (2.0 * PAIR[x + n]) * read(x if side == 0 else 7 - x, y)
                        total = value if total is None else total + value
                    at_y = pl.ds(128 * (16 * side + 8 * n - 8 + y), 128)
                    weighted[pl.ds(first, 16), at_y] = split_rows(total)

    def weigh_own(g):
        weigh(own_rows + 16 * g, lambda x, y: field[DEGREE, g, 4 + x, y])

    def weigh_other(g):
        weigh(other_rows + 16 * g, lambda x, y: other[g, x, y])

    def image_rows(g):
        local_part(DEGREE, g)
        split_into(usplit, 16 * g, range(8), lambda x, y: field[DEGREE + 1, g, 4 + x, y])
        weigh_own(g)

    lanes = lax.broadcasted_iota(jnp.int32, (8, 128), 1)
    subs = lax.broadcasted_iota(jnp.int32, (8, 128), 0)
    used = (lanes < 64) & (lax.rem(lanes, 16) < 8)

    def folded(value):
        return value + pltpu.roll(value, 120, 1)

    def packed_gram(total):
        tile[:, pl.ds(0, 64)] = total
        value = jnp.zeros((8, 128), jnp.float32)
        for q in range(4):
            row = folded(tile[pl.ds(16 * q, 8)] + tile[pl.ds(16 * q + 8, 8)])
            row = jnp.where(used, row, 0.0)
            value = value + (row if q == 0 else pltpu.roll(row, SHIFT[q], 1))
        return value

    def unpacked_gram(value):
        rows = [value] + [pltpu.roll(value, 128 - SHIFT[q], 1) for q in range(1, 4)]
        return [jnp.where(used, row, 0.0) for row in rows]

    def packed_image(total):
        tile[pl.ds(0, 8), pl.ds(0, 64)] = total[:8] + total[8:16]
        tile[pl.ds(8, 8), pl.ds(0, 64)] = total[16:24] + total[24:]
        one, two = [jnp.where(used, folded(tile[pl.ds(8 * g, 8)]), 0.0) for g in range(2)]
        both = one + pltpu.roll(two, 8, 1)
        return (both + pltpu.roll(pltpu.roll(both, 64, 1), 4, 0))[:4]

    def unpacked_image(value):
        moved = pltpu.roll(value, 64, 1)
        one = jnp.where(subs < 4, value, pltpu.roll(moved, 4, 0))
        two = jnp.where(subs < 4, pltpu.roll(value, 4, 0), moved)
        rows = [one, pltpu.roll(one, 120, 1), two, pltpu.roll(two, 120, 1)]
        return [jnp.where(used, row, 0.0) for row in rows]

    last = DEGREE - 1

    for g in range(2):
        loads[1 + g].wait()
        relayout(g)
        if g == 0:
            pl.semaphore_wait(barrier, len(nearest))
        for part in range(PARTS):
            for side in range(2):
                send(side, halo_copy(0, g, side, part))
    tell(0)
    loads[0].wait()
    for side in range(2):
        send(side, pot_copy(side))
    lax.fori_loop(0, 2 * (DEGREE + 1), clear, 0)
    tile[...] = jnp.zeros((64, 128), jnp.float32)
    lax.fori_loop(0, 8, set_weight, 0)
    for g in range(2):
        local_part(0, g)

    for s in range(last):
        for g in range(2):

            def exchange(part, carry):
                for side in range(2):

                    @pl.when(has[side])
                    def _():
                        halo_copy(s, g, side, part).wait_recv()
                        halo_part(s, g, side, part)
                        halo_copy(s + 1, g, 1 - side, part).start()

                return carry

            lax.fori_loop(0, PARTS, exchange, 0)
            local_part(s + 1, g)
        hear(s)
        tell(s + 1)
    for g in range(2):
        for side in range(2):
            send(side, far_copy(g, side))

    for side in range(2):

        @pl.when(has[side])
        def _():
            pot_copy(side).wait_recv()
            for n in range(2):
                spread_weight(weight_far.at[side, n], pot_far[side, n])

    gram = jnp.zeros((64, 64), jnp.float32)
    for g in range(2):
        for part in range(PARTS):
            for side in range(2):

                @pl.when(has[side])
                def _():
                    halo_copy(last, g, side, part).wait_recv()
                    halo_part(last, g, side, part)

            sibling_copy(g, part).start()
            split_own(g, part)
            if part > 0:
                sibling_copy(g, part - 1).wait_recv()
                split_other(g, part - 1)
                if g == 1:
                    gram = gram_part(part - 1, gram)
        image_rows(g)
        sibling_copy(g, PARTS - 1).wait_recv()
        split_other(g, PARTS - 1)
        if g == 0:
            weigh_other(0)
    hear(last)
    sum_start(0, packed_gram(gram_part(PARTS - 1, gram)))

    image = product(usplit[...], split[...])
    weigh_other(1)
    for side in range(2):

        @pl.when(has[side])
        def _():
            for g in range(2):
                far_copy(g, side).wait_recv()
                border_part(g, side)

        @pl.when(jnp.logical_not(has[side]))
        def _():
            border[:, pl.ds(2048 * side, 2048)] = jnp.zeros((32, 2048), jnp.bfloat16)

    sum_start(2, packed_image(image + product(border[...], weighted[...])))
    sum_start(1, summed(0))
    sum_start(3, summed(2))

    gram = [row * (1.0 / cells) for row in unpacked_gram(summed(1))]
    rows = [jnp.where(lanes == subs + (64 + 16 * q), 1.0, gram[q]) for q in range(4)]
    inverse = eliminated(rows, subs)
    inverse = [jnp.where(used, pltpu.roll(row, 64, 1), 0.0) for row in inverse]

    own = [jnp.where(band == 0, inverse[q], inverse[2 + q]) for q in range(2)]
    own = split_rows(jnp.concatenate([v + pltpu.roll(v, 8, 1) for v in own], 0))[:, :64]

    for part in range(PARTS):
        for x in range(8):
            at_x = pl.ds(128 * YS * (8 * part + x), 128 * YS)
            value = lax.dot_general(own, split[:, at_x], NN, preferred_element_type=jnp.float32)
            value = value[:16] + value[16:]
            for y in range(YS):
                row = x * 8 + part * YS + y
                nat[pl.ds(row, 16, stride=64), :] = value[:, 128 * y : 128 * y + 128]
    out = pltpu.make_async_copy(nat, orbitals, in_sem.at[0])
    out.start()

    dot = functools.partial(
        lax.dot_general, precision=lax.Precision.HIGHEST, preferred_element_type=jnp.float32
    )
    inverse = jnp.concatenate(inverse, 0)[:, :64]
    column = lax.broadcasted_iota(jnp.int32, (64, 32), 1)
    spread = lax.broadcasted_iota(jnp.int32, (64, 32), 0)
    spread = spread == 16 * lax.div(column, 8) + lax.rem(column, 8)
    narrow = dot(inverse, jnp.where(spread, 1.0, 0.0), NN)
    image = [(HALF_WIDTH / cells) * i + CENTER * g for i, g in zip(unpacked_image(summed(3)), gram)]
    image = jnp.concatenate(image, 0)[:, :64]
    one = dot(dot(narrow, image, NN), inverse, NT)
    two = dot(dot(inverse, image, NT), narrow, NT)
    projected[...] = 0.5 * (one + two)

    for side in range(2):

        @pl.when(has[1 - side])
        def _():
            pot_copy(side).wait_send()
            for g in range(2):
                far_copy(g, side).wait_send()
                for s in range(DEGREE):
                    for part in range(PARTS):
                        halo_copy(s, g, side, part).wait_send()

    for g in range(2):
        for part in range(PARTS):
            sibling_copy(g, part).wait_send()
    for f in range(4):
        for d in range(1, sums[f][0]):
            sum_copy(f, d).wait_send()
    out.wait()


def eliminated(rows, subs):
    def spread(value):
        return jnp.broadcast_to(value, (8, 128))

    rows = list(rows)
    for r in range(4):
        lane = 16 * r
        column = {
            q: [spread(rows[q][:, lane + b : lane + b + 1]) for b in range(8)] for q in range(r, 4)
        }
        block = [[spread(column[r][b][a : a + 1]) for b in range(a + 1)] for a in range(8)]
        pivot = [spread(rows[r][a : a + 1]) for a in range(8)]
        factor = {q: [None] * 8 for q in range(r + 1, 4)}
        for k in range(8):
            reciprocal = 1.0 / block[k][k]
            for a in range(k + 1, 8):
                ratio = block[a][k] * reciprocal
                for b in range(k + 1, a + 1):
                    block[a][b] = block[a][b] - ratio * block[b][k]
                pivot[a] = pivot[a] - ratio * pivot[k]
            for q in range(r + 1, 4):
                factor[q][k] = column[q][k] * reciprocal
                for b in range(k + 1, 8):
                    column[q][b] = column[q][b] - factor[q][k] * block[b][k]
        for q in range(r + 1, 4):
            for k in range(8):
                rows[q] = rows[q] - factor[q][k] * pivot[k]
        done = pivot[0] * lax.rsqrt(block[0][0])
        for k in range(1, 8):
            done = jnp.where(subs == k, pivot[k] * lax.rsqrt(block[k][k]), done)
        rows[r] = done
    return rows


def shards(trial_block, potential):
    rings = RINGS[lax.axis_size("dom")]
    most = max(2 * rings[2], rings[0] // 2 * rings[1])
    f32, dma = jnp.float32, pltpu.SemaphoreType.DMA
    orbitals, projected = pl.pallas_call(
        functools.partial(kernel, rings),
        out_shape=(
            jax.ShapeDtypeStruct((1024, 128), f32),
            jax.ShapeDtypeStruct((32, 32), f32),
        ),
        in_specs=[pl.BlockSpec(memory_space=pl.ANY)] * 2,
        out_specs=(
            pl.BlockSpec(memory_space=pl.ANY),
            pl.BlockSpec(memory_space=pltpu.VMEM),
        ),
        scratch_shapes=[
            pltpu.VMEM((1024, 128), f32),
            pltpu.VMEM((8, 8, 128), f32),
            pltpu.VMEM((2, 2, 8, 128), f32),
            pltpu.VMEM((8, 8, 8, 128), f32),
            pltpu.VMEM((2, 2, 8, 8, 128), f32),
            pltpu.VMEM((DEGREE + 2, 2, 16, 8, 8, 128), f32),
            pltpu.VMEM((DEGREE, 2, 2, 4, 8, 8, 128), f32),
            pltpu.VMEM((2, 2, 2, 8, 8, 128), f32),
            pltpu.VMEM((2, 8, 8, 8, 128), f32),
            pltpu.VMEM((64, 8192), jnp.bfloat16),
            pltpu.VMEM((32, 8192), jnp.bfloat16),
            pltpu.VMEM((32, 4096), jnp.bfloat16),
            pltpu.VMEM((64, 4096), jnp.bfloat16),
            pltpu.VMEM((64, 128), f32),
            pltpu.VMEM((3, most, 8, 128), f32),
            pltpu.VMEM((4 * rings[2], 4, 128), f32),
            dma((3,)),
            dma((DEGREE, 2, 2, PARTS)),
            dma((DEGREE, 2, 2, PARTS)),
            dma((3, 2)),
            dma((3, 2)),
            dma((2, PARTS)),
            dma((2, PARTS)),
            dma((4, 4 * rings[2])),
            dma((4, 4 * rings[2])),
            pltpu.SemaphoreType.REGULAR((4, 6)),
        ],
        compiler_params=pltpu.CompilerParams(
            collective_id=0, has_side_effects=True, vmem_limit_bytes=60 * 1024 * 1024
        ),
        cost_estimate=pl.CostEstimate(
            flops=200_000_000, bytes_accessed=1_100_000, transcendentals=0
        ),
    )(trial_block.reshape(1024, 128), potential)
    return orbitals.reshape(trial_block.shape), projected


def solution(mesh):
    return jax.shard_map(
        shards,
        mesh=mesh,
        in_specs=(P("band", "dom", None, None), P("dom", None, None)),
        out_specs=(P("band", "dom", None, None), P()),
        check_vma=False,
    )
```

```python
import functools

import jax
import jax.numpy as jnp
from jax import lax
from jax.experimental import pallas as pl
from jax.experimental.pallas import tpu as pltpu
from jax.sharding import PartitionSpec as P

COEFFS = (-205.0 / 72.0, 8.0 / 5.0, -1.0 / 5.0, 8.0 / 315.0, -1.0 / 560.0)
CENTER = 5.75
HALF_WIDTH = 5.25
DEGREE = 4

PAIR = tuple(-0.5 * c / HALF_WIDTH for c in COEFFS)
DIAG = -1.5 * COEFFS[0] - CENTER

MESH = pl.DeviceIdType.MESH
NT = (((1,), (1,)), ((), ()))
NN = (((1,), (0,)), ((), ()))
PARTS = 2
YS = 8 // PARTS
SHIFT = (0, 8, 64, 72)
RINGS = {256: (4, 8, 8), 8: (2, 2, 2)}


def far_first(count):
    return sorted(range(1, count), key=lambda d: -min(d, count - d))


def kernel(
    rings,
    trial,
    potential,
    orbitals,
    projected,
    nat,
    pot,
    pot_far,
    weight,
    weight_far,
    field,
    halo,
    far,
    layers,
    other,
    split,
    usplit,
    border,
    weighted,
    tile,
    slots,
    thin,
    in_sem,
    halo_send,
    halo_recv,
    far_send,
    far_recv,
    sib_send,
    sib_recv,
    red_send,
    red_recv,
    known,
):
    nx, nz, ny = rings
    doms = nx * nz * ny
    cells = doms * 8 * 8 * 128
    dom = lax.axis_index("dom")
    band = lax.axis_index("band")
    py = lax.rem(dom, ny)
    pz = lax.rem(lax.div(dom, ny), nz)
    px = lax.div(dom, ny * nz)
    left = lax.rem(dom + doms - 1, doms)
    right = lax.rem(dom + 1, doms)

    def at(x, z, y):
        return (x * nz + z) * ny + y

    pairs = nx // 2
    half = lax.div(px, 2)

    def member_yx(p):
        x = 2 * half + lax.rem(p, 2)
        return {"dom": at(x, pz, lax.div(p, 2)), "band": band}

    def member_core(p):
        return {**member_yx(lax.div(p, 2)), "band": lax.rem(p, 2)}

    def member_zx(p):
        x = jnp.where(lax.rem(p, pairs) == half, px, nx - 1 - px)
        return {"dom": at(x, lax.div(p, pairs), py), "band": band}

    place_yx = 2 * py + lax.rem(px, 2)
    along_z = (pairs * nz, pairs * pz + half, member_zx)
    sums = (
        (2 * ny, place_yx, member_yx, slots.at[0]),
        (*along_z, slots.at[1]),
        (4 * ny, 2 * place_yx + band, member_core, thin),
        (*along_z, slots.at[2]),
    )

    loads = [
        pltpu.make_async_copy(potential, pot, in_sem.at[2]),
        pltpu.make_async_copy(trial.at[pl.ds(0, 512)], nat.at[pl.ds(0, 512)], in_sem.at[0]),
        pltpu.make_async_copy(trial.at[pl.ds(512, 512)], nat.at[pl.ds(512, 512)], in_sem.at[1]),
    ]
    for load in loads:
        load.start()

    def along(axis, steps):
        where = [px, pz, py]
        size = rings[axis]
        where[axis] = lax.rem(where[axis] + steps + size, size)
        return {"dom": at(*where), "band": band}

    one_hop = [along(axis, way) for axis in range(3) for way in (1, -1)]
    two_hops = [
        along(axis, way)
        for axis in (1, 2)
        for way in (2, -2)
        if rings[axis] > 2
    ]
    sibling = {"dom": dom, "band": 1 - band}

    barrier = pltpu.get_barrier_semaphore()
    nearest = one_hop + [{"dom": d, "band": band} for d in (left, right)] + [sibling]
    for device in nearest:
        pl.semaphore_signal(barrier, inc=1, device_id=device, device_id_type=MESH)
    rounds = (one_hop, two_hops, two_hops, [sibling])

    def tell(r):
        for i, device in enumerate(rounds[r]):
            pl.semaphore_signal(
                known.at[r, i], inc=1, device_id=device, device_id_type=MESH
            )

    def hear(r):
        for i in range(len(rounds[r])):
            pl.semaphore_wait(known.at[r, i], 1)

    zeros = jnp.zeros((4, 8, 8, 128), jnp.float32)

    def clear(i, carry):
        s, g = lax.div(i, 2), lax.rem(i, 2)
        field[s, g, pl.ds(0, 4)] = zeros
        field[s, g, pl.ds(12, 4)] = zeros
        return carry

    def spread_weight(target, rows):
        rows = (rows + DIAG) * (1.0 / HALF_WIDTH)
        for y in range(8):
            target[y] = jnp.broadcast_to(rows[y : y + 1], (8, 128))

    def set_weight(x, carry):
        spread_weight(weight.at[x], pot[x])
        return carry

    def relayout(g):
        def body(x, carry):
            for y in range(8):
                field[0, g, 4 + x, y] = nat[pl.ds(g * 512 + x * 8 + y, 8, stride=64), :]
            return carry

        lax.fori_loop(0, 8, body, 0)

    has = (dom > 0, dom < doms - 1)

    def to_neighbour(side, src, dst, send_sem, recv_sem):
        return pltpu.make_async_remote_copy(
            src_ref=src,
            dst_ref=dst,
            send_sem=send_sem,
            recv_sem=recv_sem,
            device_id={"dom": right if side == 0 else left, "band": band},
            device_id_type=MESH,
        )

    def halo_copy(s, g, side, part):
        ys = pl.ds(part * YS, YS)
        return to_neighbour(
            side,
            field.at[s, g, pl.ds(8 if side == 0 else 4, 4), ys],
            halo.at[s, g, side, :, ys],
            halo_send.at[s, g, side, part],
            halo_recv.at[s, g, side, part],
        )

    def far_copy(g, side):
        return to_neighbour(
            side,
            field.at[last, g, pl.ds(6 if side == 0 else 8, 2)],
            far.at[g, side],
            far_send.at[g, side],
            far_recv.at[g, side],
        )

    def pot_copy(side):
        return to_neighbour(
            side,
            pot.at[pl.ds(6 if side == 0 else 0, 2)],
            pot_far.at[side],
            far_send.at[2, side],
            far_recv.at[2, side],
        )

    def send(side, copy):
        @pl.when(has[1 - side])
        def _():
            copy.start()

    lane = lax.broadcasted_iota(jnp.int32, (8, 8, 128), 2)

    def shifted_y(c, k):
        empty = jnp.zeros((k, 8, 128), jnp.float32)
        return jnp.concatenate([c[k:], empty], 0) + jnp.concatenate([empty, c[: 8 - k]], 0)

    def shifted_z(c, k):
        below = jnp.where(lane >= k, pltpu.roll(c, k, 2), 0.0)
        return below + jnp.where(lane < 128 - k, pltpu.roll(c, 128 - k, 2), 0.0)

    def local_part(s, g):
        def body(x, carry):
            c = field[s, g, 4 + x]
            total = weight[x] * c
            for k in range(1, 5):
                pairs = field[s, g, 4 + x + k] + field[s, g, 4 + x - k]
                pairs = pairs + shifted_y(c, k) + shifted_z(c, k)
                total = total + PAIR[k] * pairs
            if 1 <= s < DEGREE:
                total = 2.0 * total - field[s - 1, g, 4 + x]
            field[s + 1, g, 4 + x] = total
            return carry

        lax.fori_loop(0, 8, body, 0)

    def halo_part(s, g, side, part):
        twice = 1.0 if s == 0 else 2.0
        ys = pl.ds(part * YS, YS)
        cells_at = {n: halo[s, g, side, 4 - n if side == 0 else n - 1, ys] for n in range(1, 5)}
        for x in range(4):
            mine = 4 + x if side == 0 else 11 - x
            total = field[s + 1, g, mine, ys]
            for n in range(1, 5 - x):
                total = total + (twice * PAIR[x + n]) * cells_at[n]
            field[s + 1, g, mine, ys] = total

    def border_start(g, side):
        def cell(n):
            if n > 0:
                return halo[last, g, side, 4 - n if side == 0 else n - 1]
            return field[last, g, 4 - n if side == 0 else 11 + n]

        for n in (1, 2):
            c = cell(n)
            total = weight_far[side, 2 - n if side == 0 else n - 1] * c
            for k in range(1, 5):
                near = cell(n - k) + shifted_y(c, k) + shifted_z(c, k)
                if n + k < 5:
                    near = near + cell(n + k)
                total = total + PAIR[k] * near
            total = 2.0 * total - halo[last - 1, g, side, 4 - n if side == 0 else n - 1]
            layers[g, side, n - 1] = total

    def border_end(g, side):
        five, six = [far[g, side, 6 - n if side == 0 else n - 5] for n in (5, 6)]
        split_layer(side, 1, g, layers[g, side, 0] + (2.0 * PAIR[4]) * five)
        total = layers[g, side, 1] + (2.0 * PAIR[3]) * five
        split_layer(side, 2, g, total + (2.0 * PAIR[4]) * six)

    def sibling_copy(g, part):
        ys = pl.ds(part * YS, YS)
        return pltpu.make_async_remote_copy(
            src_ref=field.at[DEGREE, g, pl.ds(4, 8), ys],
            dst_ref=other.at[g, :, ys],
            send_sem=sib_send.at[g, part],
            recv_sem=sib_recv.at[g, part],
            device_id={"dom": dom, "band": 1 - band},
            device_id_type=MESH,
        )

    def sum_copy(f, d):
        count, place, member, into = sums[f]
        return pltpu.make_async_remote_copy(
            src_ref=into.at[place],
            dst_ref=into.at[place],
            send_sem=red_send.at[f],
            recv_sem=red_recv.at[f],
            device_id=member(lax.rem(place + d, count)),
            device_id_type=MESH,
        )

    def sum_start(f, value):
        count, place, _, into = sums[f]
        into[place] = value
        for d in far_first(count):
            sum_copy(f, d).start()

    def sum_tiles(f):
        count, place, member, into = sums[f]
        tiles = into.at[pl.ds(0, count - 1)]
        return pltpu.make_async_remote_copy(
            src_ref=tiles,
            dst_ref=tiles,
            send_sem=red_send.at[f],
            recv_sem=red_recv.at[f],
            device_id=member(lax.rem(place + 1, count)),
            device_id_type=MESH,
        )

    def summed(f):
        count, _, _, into = sums[f]
        sum_tiles(f).wait_recv()
        step = 2 if f == 2 else 1
        totals = []
        for first in range(step):
            total = into[first]
            for p in range(first + step, count, step):
                total = total + into[p]
            totals.append(total)
        return jnp.concatenate(totals, 0)

    def split_rows(value):
        high = value.astype(jnp.bfloat16).astype(jnp.float32)
        return jnp.concatenate([high, value - high], 0).astype(jnp.bfloat16)

    def lanes_at(x, y):
        return pl.ds(128 * (8 * YS * (y // YS) + YS * x + y % YS), 128)

    def split_into(target, first, ys, read):
        for x in range(8):
            for y in ys:
                target[pl.ds(first, 16), lanes_at(x, y)] = split_rows(read(x, y))

    own_rows = pl.multiple_of(band * 32, 32)
    other_rows = pl.multiple_of(32 - band * 32, 32)

    def of_part(part):
        return range(part * YS, (part + 1) * YS)

    def split_own(g, part):
        first = own_rows + 16 * g
        split_into(split, first, of_part(part), lambda x, y: field[DEGREE, g, 4 + x, y])

    def split_other(g, part):
        split_into(split, other_rows + 16 * g, of_part(part), lambda x, y: other[g, x, y])

    def product(left, right):
        return lax.dot_general(left, right, NT, preferred_element_type=jnp.float32)

    def gram_part(part, total):
        rows = split[:, pl.ds(part * YS * 1024, YS * 1024)]
        return total + product(rows, rows)

    def split_layer(side, n, g, value):
        for y in range(8):
            at_y = pl.ds(128 * (16 * side + 8 * n - 8 + y), 128)
            border[pl.ds(16 * g, 16), at_y] = split_rows(value[y])

    def weigh(first, read):
        for side in range(2):
            for n in (1, 2):
                for y in range(8):
                    total = None
                    for x in range(0 if side == 0 else 2, 5 - n):
                        value = (2.0 * PAIR[x + n]) * read(x if side == 0 else 7 - x, y)
                        total = value if total is None else total + value
                    at_y = pl.ds(128 * (16 * side + 8 * n - 8 + y), 128)
                    weighted[pl.ds(first, 16), at_y] = split_rows(total)

    def weigh_own(g):
        weigh(own_rows + 16 * g, lambda x, y: field[DEGREE, g, 4 + x, y])

    def weigh_other(g):
        weigh(other_rows + 16 * g, lambda x, y: other[g, x, y])

    def image_rows(g):
        local_part(DEGREE, g)
        split_into(usplit, 16 * g, range(8), lambda x, y: field[DEGREE + 1, g, 4 + x, y])
        weigh_own(g)
        for side in range(2):
            pl.when(has[side])(functools.partial(border_start, g, side))

    lanes = lax.broadcasted_iota(jnp.int32, (8, 128), 1)
    subs = lax.broadcasted_iota(jnp.int32, (8, 128), 0)
    used = (lanes < 64) & (lax.rem(lanes, 16) < 8)

    def folded(value):
        return value + pltpu.roll(value, 120, 1)

    def packed_gram(total):
        tile[:, pl.ds(0, 64)] = total
        value = jnp.zeros((8, 128), jnp.float32)
        for q in range(4):
            row = folded(tile[pl.ds(16 * q, 8)] + tile[pl.ds(16 * q + 8, 8)])
            row = jnp.where(used, row, 0.0)
            value = value + (row if q == 0 else pltpu.roll(row, SHIFT[q], 1))
        return value

    def unpacked_gram(value):
        rows = [value] + [pltpu.roll(value, 128 - SHIFT[q], 1) for q in range(1, 4)]
        return [jnp.where(used, row, 0.0) for row in rows]

    def packed_image(total):
        tile[pl.ds(0, 8), pl.ds(0, 64)] = total[:8] + total[8:16]
        tile[pl.ds(8, 8), pl.ds(0, 64)] = total[16:24] + total[24:]
        one, two = [jnp.where(used, folded(tile[pl.ds(8 * g, 8)]), 0.0) for g in range(2)]
        both = one + pltpu.roll(two, 8, 1)
        return (both + pltpu.roll(pltpu.roll(both, 64, 1), 4, 0))[:4]

    def unpacked_image(value):
        moved = pltpu.roll(value, 64, 1)
        one = jnp.where(subs < 4, value, pltpu.roll(moved, 4, 0))
        two = jnp.where(subs < 4, pltpu.roll(value, 4, 0), moved)
        rows = [one, pltpu.roll(one, 120, 1), two, pltpu.roll(two, 120, 1)]
        return [jnp.where(used, row, 0.0) for row in rows]

    last = DEGREE - 1

    for g in range(2):
        loads[1 + g].wait()
        relayout(g)
        if g == 0:
            pl.semaphore_wait(barrier, len(nearest))
        for part in range(PARTS):
            for side in range(2):
                send(side, halo_copy(0, g, side, part))
    tell(0)
    loads[0].wait()
    for side in range(2):
        send(side, pot_copy(side))
    lax.fori_loop(0, 2 * (DEGREE + 1), clear, 0)
    tile[...] = jnp.zeros((64, 128), jnp.float32)
    lax.fori_loop(0, 8, set_weight, 0)
    for g in range(2):
        local_part(0, g)

    for s in range(last):
        for g in range(2):

            def exchange(part, carry):
                for side in range(2):

                    @pl.when(has[side])
                    def _():
                        halo_copy(s, g, side, part).wait_recv()
                        halo_part(s, g, side, part)
                        halo_copy(s + 1, g, 1 - side, part).start()

                return carry

            lax.fori_loop(0, PARTS, exchange, 0)
            local_part(s + 1, g)
        hear(s)
        tell(s + 1)
    for g in range(2):
        for side in range(2):
            send(side, far_copy(g, side))

    for side in range(2):

        @pl.when(has[side])
        def _():
            pot_copy(side).wait_recv()
            for n in range(2):
                spread_weight(weight_far.at[side, n], pot_far[side, n])

    gram = jnp.zeros((64, 64), jnp.float32)
    for g in range(2):
        for part in range(PARTS):
            for side in range(2):

                @pl.when(has[side])
                def _():
                    halo_copy(last, g, side, part).wait_recv()
                    halo_part(last, g, side, part)

            sibling_copy(g, part).start()
            split_own(g, part)
            if part > 0:
                sibling_copy(g, part - 1).wait_recv()
                split_other(g, part - 1)
                if g == 1:
                    gram = gram_part(part - 1, gram)
        image_rows(g)
        sibling_copy(g, PARTS - 1).wait_recv()
        split_other(g, PARTS - 1)
        if g == 0:
            weigh_other(0)
    hear(last)
    sum_start(0, packed_gram(gram_part(PARTS - 1, gram)))

    image = product(usplit[...], split[...])
    weigh_other(1)
    for g in range(2):
        for side in range(2):

            @pl.when(has[side])
            def _():
                far_copy(g, side).wait_recv()
                border_end(g, side)

    for side in range(2):

        @pl.when(jnp.logical_not(has[side]))
        def _():
            border[:, pl.ds(2048 * side, 2048)] = jnp.zeros((32, 2048), jnp.bfloat16)

    sum_start(2, packed_image(image + product(border[...], weighted[...])))
    sum_start(1, summed(0))
    sum_start(3, summed(2))

    gram = [row * (1.0 / cells) for row in unpacked_gram(summed(1))]
    rows = [jnp.where(lanes == subs + (64 + 16 * q), 1.0, gram[q]) for q in range(4)]
    inverse = eliminated(rows, subs)
    inverse = [jnp.where(used, pltpu.roll(row, 64, 1), 0.0) for row in inverse]

    own = [jnp.where(band == 0, inverse[q], inverse[2 + q]) for q in range(2)]
    own = split_rows(jnp.concatenate([v + pltpu.roll(v, 8, 1) for v in own], 0))[:, :64]

    for part in range(PARTS):
        for x in range(8):
            at_x = pl.ds(128 * YS * (8 * part + x), 128 * YS)
            value = lax.dot_general(own, split[:, at_x], NN, preferred_element_type=jnp.float32)
            value = value[:16] + value[16:]
            for y in range(YS):
                row = x * 8 + part * YS + y
                nat[pl.ds(row, 16, stride=64), :] = value[:, 128 * y : 128 * y + 128]
    out = pltpu.make_async_copy(nat, orbitals, in_sem.at[0])
    out.start()

    dot = functools.partial(
        lax.dot_general, precision=lax.Precision.HIGHEST, preferred_element_type=jnp.float32
    )
    inverse = jnp.concatenate(inverse, 0)[:, :64]
    column = lax.broadcasted_iota(jnp.int32, (64, 32), 1)
    spread = lax.broadcasted_iota(jnp.int32, (64, 32), 0)
    spread = spread == 16 * lax.div(column, 8) + lax.rem(column, 8)
    narrow = dot(inverse, jnp.where(spread, 1.0, 0.0), NN)
    for side in range(2):

        @pl.when(has[1 - side])
        def _():
            pot_copy(side).wait_send()
            for g in range(2):
                far_copy(g, side).wait_send()
                for s in range(DEGREE):
                    for part in range(PARTS):
                        halo_copy(s, g, side, part).wait_send()

    for g in range(2):
        for part in range(PARTS):
            sibling_copy(g, part).wait_send()
    for f in range(4):
        sum_tiles(f).wait_send()

    image = [(HALF_WIDTH / cells) * i + CENTER * g for i, g in zip(unpacked_image(summed(3)), gram)]
    image = jnp.concatenate(image, 0)[:, :64]
    one = dot(dot(narrow, image, NN), inverse, NT)
    two = dot(dot(inverse, image, NT), narrow, NT)
    projected[...] = 0.5 * (one + two)

    out.wait()


def eliminated(rows, subs):
    def spread(value):
        return jnp.broadcast_to(value, (8, 128))

    rows = list(rows)
    for r in range(4):
        lane = 16 * r
        column = {
            q: [spread(rows[q][:, lane + b : lane + b + 1]) for b in range(8)] for q in range(r, 4)
        }
        block = [[spread(column[r][b][a : a + 1]) for b in range(a + 1)] for a in range(8)]
        pivot = [spread(rows[r][a : a + 1]) for a in range(8)]
        factor = {q: [None] * 8 for q in range(r + 1, 4)}
        for k in range(8):
            reciprocal = 1.0 / block[k][k]
            for a in range(k + 1, 8):
                ratio = block[a][k] * reciprocal
                for b in range(k + 1, a + 1):
                    block[a][b] = block[a][b] - ratio * block[b][k]
                pivot[a] = pivot[a] - ratio * pivot[k]
            for q in range(r + 1, 4):
                factor[q][k] = column[q][k] * reciprocal
                for b in range(k + 1, 8):
                    column[q][b] = column[q][b] - factor[q][k] * block[b][k]
        for q in range(r + 1, 4):
            for k in range(8):
                rows[q] = rows[q] - factor[q][k] * pivot[k]
        done = pivot[0] * lax.rsqrt(block[0][0])
        for k in range(1, 8):
            done = jnp.where(subs == k, pivot[k] * lax.rsqrt(block[k][k]), done)
        rows[r] = done
    return rows


def shards(trial_block, potential):
    rings = RINGS[lax.axis_size("dom")]
    most = max(2 * rings[2], rings[0] // 2 * rings[1])
    f32, dma = jnp.float32, pltpu.SemaphoreType.DMA
    orbitals, projected = pl.pallas_call(
        functools.partial(kernel, rings),
        out_shape=(
            jax.ShapeDtypeStruct((1024, 128), f32),
            jax.ShapeDtypeStruct((32, 32), f32),
        ),
        in_specs=[pl.BlockSpec(memory_space=pl.ANY)] * 2,
        out_specs=(
            pl.BlockSpec(memory_space=pl.ANY),
            pl.BlockSpec(memory_space=pltpu.VMEM),
        ),
        scratch_shapes=[
            pltpu.VMEM((1024, 128), f32),
            pltpu.VMEM((8, 8, 128), f32),
            pltpu.VMEM((2, 2, 8, 128), f32),
            pltpu.VMEM((8, 8, 8, 128), f32),
            pltpu.VMEM((2, 2, 8, 8, 128), f32),
            pltpu.VMEM((DEGREE + 2, 2, 16, 8, 8, 128), f32),
            pltpu.VMEM((DEGREE, 2, 2, 4, 8, 8, 128), f32),
            pltpu.VMEM((2, 2, 2, 8, 8, 128), f32),
            pltpu.VMEM((2, 2, 2, 8, 8, 128), f32),
            pltpu.VMEM((2, 8, 8, 8, 128), f32),
            pltpu.VMEM((64, 8192), jnp.bfloat16),
            pltpu.VMEM((32, 8192), jnp.bfloat16),
            pltpu.VMEM((32, 4096), jnp.bfloat16),
            pltpu.VMEM((64, 4096), jnp.bfloat16),
            pltpu.VMEM((64, 128), f32),
            pltpu.VMEM((3, most, 8, 128), f32),
            pltpu.VMEM((4 * rings[2], 4, 128), f32),
            dma((3,)),
            dma((DEGREE, 2, 2, PARTS)),
            dma((DEGREE, 2, 2, PARTS)),
            dma((3, 2)),
            dma((3, 2)),
            dma((2, PARTS)),
            dma((2, PARTS)),
            dma((4,)),
            dma((4,)),
            pltpu.SemaphoreType.REGULAR((4, 6)),
        ],
        compiler_params=pltpu.CompilerParams(
            collective_id=0, has_side_effects=True, vmem_limit_bytes=60 * 1024 * 1024
        ),
        cost_estimate=pl.CostEstimate(
            flops=200_000_000, bytes_accessed=1_100_000, transcendentals=0
        ),
    )(trial_block.reshape(1024, 128), potential)
    return orbitals.reshape(trial_block.shape), projected


def solution(mesh):
    return jax.shard_map(
        shards,
        mesh=mesh,
        in_specs=(P("band", "dom", None, None), P("dom", None, None)),
        out_specs=(P("band", "dom", None, None), P()),
        check_vma=False,
    )
```

```python
import functools

import jax
import jax.numpy as jnp
from jax import lax
from jax.experimental import pallas as pl
from jax.experimental.pallas import tpu as pltpu
from jax.sharding import PartitionSpec as P

COEFFS = (-205.0 / 72.0, 8.0 / 5.0, -1.0 / 5.0, 8.0 / 315.0, -1.0 / 560.0)
CENTER = 5.75
HALF_WIDTH = 5.25
DEGREE = 4

PAIR = tuple(-0.5 * c / HALF_WIDTH for c in COEFFS)
DIAG = -1.5 * COEFFS[0] - CENTER

MESH = pl.DeviceIdType.MESH
NT = (((1,), (1,)), ((), ()))
NN = (((1,), (0,)), ((), ()))
PARTS = 2
YS = 8 // PARTS
SHIFT = (0, 8, 64, 72)
CHUNKS = 2
RINGS = {256: (4, 8, 8), 8: (2, 2, 2)}


def far_first(count):
    return sorted(range(1, count), key=lambda d: -min(d, count - d))


def kernel(
    rings,
    trial,
    potential,
    orbitals,
    projected,
    nat,
    pot,
    pot_far,
    weight,
    weight_far,
    field,
    halo,
    far,
    layers,
    other,
    split,
    usplit,
    border,
    weighted,
    tile,
    slots,
    thin,
    in_sem,
    halo_send,
    halo_recv,
    far_send,
    far_recv,
    sib_send,
    sib_recv,
    red_send,
    red_recv,
    known,
):
    nx, nz, ny = rings
    doms = nx * nz * ny
    cells = doms * 8 * 8 * 128
    dom = lax.axis_index("dom")
    band = lax.axis_index("band")
    py = lax.rem(dom, ny)
    pz = lax.rem(lax.div(dom, ny), nz)
    px = lax.div(dom, ny * nz)
    left = lax.rem(dom + doms - 1, doms)
    right = lax.rem(dom + 1, doms)

    def at(x, z, y):
        return (x * nz + z) * ny + y

    pairs = nx // 2
    half = lax.div(px, 2)

    def member_yx(p):
        x = 2 * half + lax.rem(p, 2)
        return {"dom": at(x, pz, lax.div(p, 2)), "band": band}

    def member_core(p):
        return {**member_yx(lax.div(p, 2)), "band": lax.rem(p, 2)}

    def member_zx(p):
        x = jnp.where(lax.rem(p, pairs) == half, px, nx - 1 - px)
        return {"dom": at(x, lax.div(p, pairs), py), "band": band}

    place_yx = 2 * py + lax.rem(px, 2)
    along_z = (pairs * nz, pairs * pz + half, member_zx)
    sums = (
        (2 * ny, place_yx, member_yx, slots.at[0]),
        (*along_z, slots.at[1]),
        (4 * ny, 2 * place_yx + band, member_core, thin),
        (*along_z, slots.at[2]),
    )

    loads = [
        pltpu.make_async_copy(potential, pot, in_sem.at[2]),
        pltpu.make_async_copy(trial.at[pl.ds(0, 512)], nat.at[pl.ds(0, 512)], in_sem.at[0]),
        pltpu.make_async_copy(trial.at[pl.ds(512, 512)], nat.at[pl.ds(512, 512)], in_sem.at[1]),
    ]
    for load in loads:
        load.start()

    def along(axis, steps):
        where = [px, pz, py]
        size = rings[axis]
        where[axis] = lax.rem(where[axis] + steps + size, size)
        return {"dom": at(*where), "band": band}

    one_hop = [along(axis, way) for axis in range(3) for way in (1, -1)]
    two_hops = [
        along(axis, way)
        for axis in (1, 2)
        for way in (2, -2)
        if rings[axis] > 2
    ]
    sibling = {"dom": dom, "band": 1 - band}

    barrier = pltpu.get_barrier_semaphore()
    nearest = one_hop + [{"dom": d, "band": band} for d in (left, right)] + [sibling]
    for device in nearest:
        pl.semaphore_signal(barrier, inc=1, device_id=device, device_id_type=MESH)
    rounds = (one_hop, two_hops, two_hops, [sibling])

    def tell(r):
        for i, device in enumerate(rounds[r]):
            pl.semaphore_signal(
                known.at[r, i], inc=1, device_id=device, device_id_type=MESH
            )

    def hear(r):
        for i in range(len(rounds[r])):
            pl.semaphore_wait(known.at[r, i], 1)

    zeros = jnp.zeros((4, 8, 8, 128), jnp.float32)

    def clear(i, carry):
        s, g = lax.div(i, 2), lax.rem(i, 2)
        field[s, g, pl.ds(0, 4)] = zeros
        field[s, g, pl.ds(12, 4)] = zeros
        return carry

    def spread_weight(target, rows):
        rows = (rows + DIAG) * (1.0 / HALF_WIDTH)
        for y in range(8):
            target[y] = jnp.broadcast_to(rows[y : y + 1], (8, 128))

    def set_weight(x, carry):
        spread_weight(weight.at[x], pot[x])
        return carry

    def relayout(g):
        def body(x, carry):
            for y in range(8):
                field[0, g, 4 + x, y] = nat[pl.ds(g * 512 + x * 8 + y, 8, stride=64), :]
            return carry

        lax.fori_loop(0, 8, body, 0)

    has = (dom > 0, dom < doms - 1)

    def to_neighbour(side, src, dst, send_sem, recv_sem):
        return pltpu.make_async_remote_copy(
            src_ref=src,
            dst_ref=dst,
            send_sem=send_sem,
            recv_sem=recv_sem,
            device_id={"dom": right if side == 0 else left, "band": band},
            device_id_type=MESH,
        )

    def halo_copy(s, g, side, part):
        ys = pl.ds(part * YS, YS)
        return to_neighbour(
            side,
            field.at[s, g, pl.ds(8 if side == 0 else 4, 4), ys],
            halo.at[s, g, side, :, ys],
            halo_send.at[s, g, side, part],
            halo_recv.at[s, g, side, part],
        )

    def far_copy(g, side):
        return to_neighbour(
            side,
            field.at[last, g, pl.ds(6 if side == 0 else 8, 2)],
            far.at[g, side],
            far_send.at[g, side],
            far_recv.at[g, side],
        )

    def pot_copy(side):
        return to_neighbour(
            side,
            pot.at[pl.ds(6 if side == 0 else 0, 2)],
            pot_far.at[side],
            far_send.at[2, side],
            far_recv.at[2, side],
        )

    def send(side, copy):
        @pl.when(has[1 - side])
        def _():
            copy.start()

    lane = lax.broadcasted_iota(jnp.int32, (8, 8, 128), 2)

    def shifted_y(c, k):
        empty = jnp.zeros((k, 8, 128), jnp.float32)
        return jnp.concatenate([c[k:], empty], 0) + jnp.concatenate([empty, c[: 8 - k]], 0)

    def shifted_z(c, k):
        below = jnp.where(lane >= k, pltpu.roll(c, k, 2), 0.0)
        return below + jnp.where(lane < 128 - k, pltpu.roll(c, 128 - k, 2), 0.0)

    def local_part(s, g):
        def body(x, carry):
            c = field[s, g, 4 + x]
            total = weight[x] * c
            for k in range(1, 5):
                pairs = field[s, g, 4 + x + k] + field[s, g, 4 + x - k]
                pairs = pairs + shifted_y(c, k) + shifted_z(c, k)
                total = total + PAIR[k] * pairs
            if 1 <= s < DEGREE:
                total = 2.0 * total - field[s - 1, g, 4 + x]
            field[s + 1, g, 4 + x] = total
            return carry

        lax.fori_loop(0, 8, body, 0, unroll=True)

    def halo_part(s, g, side, part):
        twice = 1.0 if s == 0 else 2.0
        ys = pl.ds(part * YS, YS)
        cells_at = {n: halo[s, g, side, 4 - n if side == 0 else n - 1, ys] for n in range(1, 5)}
        for x in range(4):
            mine = 4 + x if side == 0 else 11 - x
            total = field[s + 1, g, mine, ys]
            for n in range(1, 5 - x):
                total = total + (twice * PAIR[x + n]) * cells_at[n]
            field[s + 1, g, mine, ys] = total

    def border_start(g, side):
        def cell(n):
            if n > 0:
                return halo[last, g, side, 4 - n if side == 0 else n - 1]
            return field[last, g, 4 - n if side == 0 else 11 + n]

        for n in (1, 2):
            c = cell(n)
            total = weight_far[side, 2 - n if side == 0 else n - 1] * c
            for k in range(1, 5):
                near = cell(n - k) + shifted_y(c, k) + shifted_z(c, k)
                if n + k < 5:
                    near = near + cell(n + k)
                total = total + PAIR[k] * near
            total = 2.0 * total - halo[last - 1, g, side, 4 - n if side == 0 else n - 1]
            layers[g, side, n - 1] = total

    def border_end(g, side):
        five, six = [far[g, side, 6 - n if side == 0 else n - 5] for n in (5, 6)]
        split_layer(side, 1, g, layers[g, side, 0] + (2.0 * PAIR[4]) * five)
        total = layers[g, side, 1] + (2.0 * PAIR[3]) * five
        split_layer(side, 2, g, total + (2.0 * PAIR[4]) * six)

    def sibling_copy(g, part):
        ys = pl.ds(part * YS, YS)
        return pltpu.make_async_remote_copy(
            src_ref=field.at[DEGREE, g, pl.ds(4, 8), ys],
            dst_ref=other.at[g, :, ys],
            send_sem=sib_send.at[g, part],
            recv_sem=sib_recv.at[g, part],
            device_id={"dom": dom, "band": 1 - band},
            device_id_type=MESH,
        )

    def sum_copy(f, d):
        count, place, member, into = sums[f]
        return pltpu.make_async_remote_copy(
            src_ref=into.at[place],
            dst_ref=into.at[place],
            send_sem=red_send.at[f],
            recv_sem=red_recv.at[f],
            device_id=member(lax.rem(place + d, count)),
            device_id_type=MESH,
        )

    def sum_start(f, value):
        count, place, _, into = sums[f]
        into[place] = value
        for d in far_first(count):
            sum_copy(f, d).start()

    def sum_tiles(f):
        count, place, member, into = sums[f]
        tiles = into.at[pl.ds(0, count - 1)]
        return pltpu.make_async_remote_copy(
            src_ref=tiles,
            dst_ref=tiles,
            send_sem=red_send.at[f],
            recv_sem=red_recv.at[f],
            device_id=member(lax.rem(place + 1, count)),
            device_id_type=MESH,
        )

    def summed(f):
        count, _, _, into = sums[f]
        sum_tiles(f).wait_recv()
        step = 2 if f == 2 else 1
        totals = []
        for first in range(step):
            total = into[first]
            for p in range(first + step, count, step):
                total = total + into[p]
            totals.append(total)
        return jnp.concatenate(totals, 0)

    def split_rows(value):
        high = value.astype(jnp.bfloat16).astype(jnp.float32)
        return jnp.concatenate([high, value - high], 0).astype(jnp.bfloat16)

    def lanes_at(x, y):
        return pl.ds(128 * (8 * YS * (y // YS) + YS * x + y % YS), 128)

    def split_into(target, first, ys, read):
        for x in range(8):
            for y in ys:
                target[pl.ds(first, 16), lanes_at(x, y)] = split_rows(read(x, y))

    own_rows = pl.multiple_of(band * 32, 32)
    other_rows = pl.multiple_of(32 - band * 32, 32)

    def of_part(part):
        return range(part * YS, (part + 1) * YS)

    def split_own(g, part):
        first = own_rows + 16 * g
        split_into(split, first, of_part(part), lambda x, y: field[DEGREE, g, 4 + x, y])

    def split_other(g, part):
        split_into(split, other_rows + 16 * g, of_part(part), lambda x, y: other[g, x, y])

    def product(left, right):
        return lax.dot_general(left, right, NT, preferred_element_type=jnp.float32)

    def gram_part(part, total):
        rows = split[:, pl.ds(part * YS * 1024, YS * 1024)]
        return total + product(rows, rows)

    def split_layer(side, n, g, value):
        for y in range(8):
            at_y = pl.ds(128 * (16 * side + 8 * n - 8 + y), 128)
            border[pl.ds(16 * g, 16), at_y] = split_rows(value[y])

    def weigh(first, read):
        for side in range(2):
            for n in (1, 2):
                for y in range(8):
                    total = None
                    for x in range(0 if side == 0 else 2, 5 - n):
                        value = (2.0 * PAIR[x + n]) * read(x if side == 0 else 7 - x, y)
                        total = value if total is None else total + value
                    at_y = pl.ds(128 * (16 * side + 8 * n - 8 + y), 128)
                    weighted[pl.ds(first, 16), at_y] = split_rows(total)

    def weigh_own(g):
        weigh(own_rows + 16 * g, lambda x, y: field[DEGREE, g, 4 + x, y])

    def weigh_other(g):
        weigh(other_rows + 16 * g, lambda x, y: other[g, x, y])

    def image_rows(g):
        local_part(DEGREE, g)
        split_into(usplit, 16 * g, range(8), lambda x, y: field[DEGREE + 1, g, 4 + x, y])
        weigh_own(g)
        for side in range(2):
            pl.when(has[side])(functools.partial(border_start, g, side))

    lanes = lax.broadcasted_iota(jnp.int32, (8, 128), 1)
    subs = lax.broadcasted_iota(jnp.int32, (8, 128), 0)
    used = (lanes < 64) & (lax.rem(lanes, 16) < 8)

    def folded(value):
        return value + pltpu.roll(value, 120, 1)

    def packed_gram(total):
        tile[:, pl.ds(0, 64)] = total
        value = jnp.zeros((8, 128), jnp.float32)
        for q in range(4):
            row = folded(tile[pl.ds(16 * q, 8)] + tile[pl.ds(16 * q + 8, 8)])
            row = jnp.where(used, row, 0.0)
            value = value + (row if q == 0 else pltpu.roll(row, SHIFT[q], 1))
        return value

    def unpacked_gram(value):
        rows = [value] + [pltpu.roll(value, 128 - SHIFT[q], 1) for q in range(1, 4)]
        return [jnp.where(used, row, 0.0) for row in rows]

    def packed_image(total):
        tile[pl.ds(0, 8), pl.ds(0, 64)] = total[:8] + total[8:16]
        tile[pl.ds(8, 8), pl.ds(0, 64)] = total[16:24] + total[24:]
        one, two = [jnp.where(used, folded(tile[pl.ds(8 * g, 8)]), 0.0) for g in range(2)]
        both = one + pltpu.roll(two, 8, 1)
        return (both + pltpu.roll(pltpu.roll(both, 64, 1), 4, 0))[:4]

    def unpacked_image(value):
        moved = pltpu.roll(value, 64, 1)
        one = jnp.where(subs < 4, value, pltpu.roll(moved, 4, 0))
        two = jnp.where(subs < 4, pltpu.roll(value, 4, 0), moved)
        rows = [one, pltpu.roll(one, 120, 1), two, pltpu.roll(two, 120, 1)]
        return [jnp.where(used, row, 0.0) for row in rows]

    last = DEGREE - 1

    for g in range(2):
        loads[1 + g].wait()
        relayout(g)
    pl.semaphore_wait(barrier, len(nearest))
    for g in range(2):
        for part in range(PARTS):
            for side in range(2):
                send(side, halo_copy(0, g, side, part))
    tell(0)
    loads[0].wait()
    for side in range(2):
        send(side, pot_copy(side))
    lax.fori_loop(0, 2 * (DEGREE + 1), clear, 0)
    tile[...] = jnp.zeros((64, 128), jnp.float32)
    lax.fori_loop(0, 8, set_weight, 0)
    for g in range(2):
        local_part(0, g)

    for s in range(last):
        for g in range(2):

            def exchange(part, carry):
                for side in range(2):

                    @pl.when(has[side])
                    def _():
                        halo_copy(s, g, side, part).wait_recv()
                        halo_part(s, g, side, part)
                        halo_copy(s + 1, g, 1 - side, part).start()

                return carry

            lax.fori_loop(0, PARTS, exchange, 0)
            local_part(s + 1, g)
        hear(s)
        tell(s + 1)
    for g in range(2):
        for side in range(2):
            send(side, far_copy(g, side))

    for side in range(2):

        @pl.when(has[side])
        def _():
            pot_copy(side).wait_recv()
            for n in range(2):
                spread_weight(weight_far.at[side, n], pot_far[side, n])

    gram = jnp.zeros((64, 64), jnp.float32)
    for g in range(2):
        for part in range(PARTS):
            for side in range(2):

                @pl.when(has[side])
                def _():
                    halo_copy(last, g, side, part).wait_recv()
                    halo_part(last, g, side, part)

            sibling_copy(g, part).start()
            split_own(g, part)
            if part > 0:
                sibling_copy(g, part - 1).wait_recv()
                split_other(g, part - 1)
                if g == 1:
                    gram = gram_part(part - 1, gram)
        image_rows(g)
        sibling_copy(g, PARTS - 1).wait_recv()
        split_other(g, PARTS - 1)
        if g == 0:
            weigh_other(0)
    hear(last)
    sum_start(0, packed_gram(gram_part(PARTS - 1, gram)))

    image = product(usplit[...], split[...])
    weigh_other(1)
    for g in range(2):
        for side in range(2):

            @pl.when(has[side])
            def _():
                far_copy(g, side).wait_recv()
                border_end(g, side)

    for side in range(2):

        @pl.when(jnp.logical_not(has[side]))
        def _():
            border[:, pl.ds(2048 * side, 2048)] = jnp.zeros((32, 2048), jnp.bfloat16)

    sum_start(2, packed_image(image + product(border[...], weighted[...])))
    sum_start(1, summed(0))
    sum_start(3, summed(2))

    gram = [row * (1.0 / cells) for row in unpacked_gram(summed(1))]
    rows = [jnp.where(lanes == subs + (64 + 16 * q), 1.0, gram[q]) for q in range(4)]
    inverse = eliminated(rows, subs)
    inverse = [jnp.where(used, pltpu.roll(row, 64, 1), 0.0) for row in inverse]

    own = [jnp.where(band == 0, inverse[q], inverse[2 + q]) for q in range(2)]
    own = split_rows(jnp.concatenate([v + pltpu.roll(v, 8, 1) for v in own], 0))[:, :64]

    for part in range(PARTS):
        for x in range(8):
            at_x = pl.ds(128 * YS * (8 * part + x), 128 * YS)
            value = lax.dot_general(own, split[:, at_x], NN, preferred_element_type=jnp.float32)
            value = value[:16] + value[16:]
            for y in range(YS):
                row = x * 8 + part * YS + y
                nat[pl.ds(row, 16, stride=64), :] = value[:, 128 * y : 128 * y + 128]
    out = pltpu.make_async_copy(nat, orbitals, in_sem.at[0])
    out.start()

    dot = functools.partial(
        lax.dot_general, precision=lax.Precision.HIGHEST, preferred_element_type=jnp.float32
    )
    inverse = jnp.concatenate(inverse, 0)[:, :64]
    column = lax.broadcasted_iota(jnp.int32, (64, 32), 1)
    spread = lax.broadcasted_iota(jnp.int32, (64, 32), 0)
    spread = spread == 16 * lax.div(column, 8) + lax.rem(column, 8)
    narrow = dot(inverse, jnp.where(spread, 1.0, 0.0), NN)
    for side in range(2):

        @pl.when(has[1 - side])
        def _():
            pot_copy(side).wait_send()
            for g in range(2):
                far_copy(g, side).wait_send()
                for s in range(DEGREE):
                    for part in range(PARTS):
                        halo_copy(s, g, side, part).wait_send()

    for g in range(2):
        for part in range(PARTS):
            sibling_copy(g, part).wait_send()
    for f in range(4):
        sum_tiles(f).wait_send()

    image = [(HALF_WIDTH / cells) * i + CENTER * g for i, g in zip(unpacked_image(summed(3)), gram)]
    image = jnp.concatenate(image, 0)[:, :64]
    one = dot(dot(narrow, image, NN), inverse, NT)
    two = dot(dot(inverse, image, NT), narrow, NT)
    projected[...] = 0.5 * (one + two)

    out.wait()


def eliminated(rows, subs):
    def spread(value):
        return jnp.broadcast_to(value, (8, 128))

    rows = list(rows)
    for r in range(4):
        lane = 16 * r
        column = {
            q: [spread(rows[q][:, lane + b : lane + b + 1]) for b in range(8)] for q in range(r, 4)
        }
        block = [[spread(column[r][b][a : a + 1]) for b in range(a + 1)] for a in range(8)]
        pivot = [spread(rows[r][a : a + 1]) for a in range(8)]
        factor = {q: [None] * 8 for q in range(r + 1, 4)}
        for k in range(8):
            reciprocal = 1.0 / block[k][k]
            for a in range(k + 1, 8):
                ratio = block[a][k] * reciprocal
                for b in range(k + 1, a + 1):
                    block[a][b] = block[a][b] - ratio * block[b][k]
                pivot[a] = pivot[a] - ratio * pivot[k]
            for q in range(r + 1, 4):
                factor[q][k] = column[q][k] * reciprocal
                for b in range(k + 1, 8):
                    column[q][b] = column[q][b] - factor[q][k] * block[b][k]
        for q in range(r + 1, 4):
            for k in range(8):
                rows[q] = rows[q] - factor[q][k] * pivot[k]
        done = pivot[0] * lax.rsqrt(block[0][0])
        for k in range(1, 8):
            done = jnp.where(subs == k, pivot[k] * lax.rsqrt(block[k][k]), done)
        rows[r] = done
    return rows


def hand_over(orbitals, projected, orbitals_out, projected_out, rows, matrix, read_sem, write_sem):
    steps = [(projected, matrix, projected_out)]
    for i in range(CHUNKS):
        part = pl.ds(i * (1024 // CHUNKS), 1024 // CHUNKS)
        steps.append((orbitals.at[part], rows.at[part], orbitals_out.at[part]))
    reads = [pltpu.make_async_copy(a, b, read_sem.at[i]) for i, (a, b, _) in enumerate(steps)]
    writes = [pltpu.make_async_copy(b, c, write_sem.at[i]) for i, (_, b, c) in enumerate(steps)]
    for read in reads:
        read.start()
    for read, write in zip(reads, writes):
        read.wait()
        write.start()
    for write in writes:
        write.wait()


def shards(trial_block, potential):
    rings = RINGS[lax.axis_size("dom")]
    most = max(2 * rings[2], rings[0] // 2 * rings[1])
    f32, dma = jnp.float32, pltpu.SemaphoreType.DMA
    orbitals, projected = pl.pallas_call(
        functools.partial(kernel, rings),
        out_shape=(
            jax.ShapeDtypeStruct((1024, 128), f32),
            jax.ShapeDtypeStruct((32, 32), f32),
        ),
        in_specs=[pl.BlockSpec(memory_space=pl.ANY)] * 2,
        out_specs=(
            pl.BlockSpec(memory_space=pl.ANY),
            pl.BlockSpec(memory_space=pltpu.VMEM),
        ),
        scratch_shapes=[
            pltpu.VMEM((1024, 128), f32),
            pltpu.VMEM((8, 8, 128), f32),
            pltpu.VMEM((2, 2, 8, 128), f32),
            pltpu.VMEM((8, 8, 8, 128), f32),
            pltpu.VMEM((2, 2, 8, 8, 128), f32),
            pltpu.VMEM((DEGREE + 2, 2, 16, 8, 8, 128), f32),
            pltpu.VMEM((DEGREE, 2, 2, 4, 8, 8, 128), f32),
            pltpu.VMEM((2, 2, 2, 8, 8, 128), f32),
            pltpu.VMEM((2, 2, 2, 8, 8, 128), f32),
            pltpu.VMEM((2, 8, 8, 8, 128), f32),
            pltpu.VMEM((64, 8192), jnp.bfloat16),
            pltpu.VMEM((32, 8192), jnp.bfloat16),
            pltpu.VMEM((32, 4096), jnp.bfloat16),
            pltpu.VMEM((64, 4096), jnp.bfloat16),
            pltpu.VMEM((64, 128), f32),
            pltpu.VMEM((3, most, 8, 128), f32),
            pltpu.VMEM((4 * rings[2], 4, 128), f32),
            dma((3,)),
            dma((DEGREE, 2, 2, PARTS)),
            dma((DEGREE, 2, 2, PARTS)),
            dma((3, 2)),
            dma((3, 2)),
            dma((2, PARTS)),
            dma((2, PARTS)),
            dma((4,)),
            dma((4,)),
            pltpu.SemaphoreType.REGULAR((4, 6)),
        ],
        compiler_params=pltpu.CompilerParams(
            collective_id=0, has_side_effects=True, vmem_limit_bytes=60 * 1024 * 1024
        ),
        cost_estimate=pl.CostEstimate(
            flops=200_000_000, bytes_accessed=1_100_000, transcendentals=0
        ),
    )(trial_block.reshape(1024, 128), potential)
    anywhere = pl.BlockSpec(memory_space=pl.ANY)
    orbitals, projected = pl.pallas_call(
        hand_over,
        out_shape=(
            jax.ShapeDtypeStruct((1024, 128), f32),
            jax.ShapeDtypeStruct((32, 32), f32),
        ),
        in_specs=[anywhere] * 2,
        out_specs=(anywhere, anywhere),
        scratch_shapes=[
            pltpu.VMEM((1024, 128), f32),
            pltpu.VMEM((32, 32), f32),
            dma((CHUNKS + 1,)),
            dma((CHUNKS + 1,)),
        ],
        compiler_params=pltpu.CompilerParams(vmem_limit_bytes=60 * 1024 * 1024),
    )(orbitals, projected)
    return orbitals.reshape(trial_block.shape), projected


def solution(mesh):
    return jax.shard_map(
        shards,
        mesh=mesh,
        in_specs=(P("band", "dom", None, None), P("dom", None, None)),
        out_specs=(P("band", "dom", None, None), P()),
        check_vma=False,
    )
```

```python
import functools

import jax
import jax.numpy as jnp
from jax import lax
from jax.experimental import pallas as pl
from jax.experimental.pallas import tpu as pltpu
from jax.sharding import PartitionSpec as P

COEFFS = (-205.0 / 72.0, 8.0 / 5.0, -1.0 / 5.0, 8.0 / 315.0, -1.0 / 560.0)
CENTER = 5.75
HALF_WIDTH = 5.25
DEGREE = 4

PAIR = tuple(-0.5 * c / HALF_WIDTH for c in COEFFS)
DIAG = -1.5 * COEFFS[0] - CENTER

MESH = pl.DeviceIdType.MESH
NT = (((1,), (1,)), ((), ()))
NN = (((1,), (0,)), ((), ()))
PARTS = 2
YS = 8 // PARTS
SHIFT = (0, 8, 64, 72)
RINGS = {256: (4, 8, 8), 8: (2, 2, 2)}


def far_first(count):
    return sorted(range(1, count), key=lambda d: -min(d, count - d))


def kernel(
    rings,
    trial,
    potential,
    orbitals,
    projected,
    nat,
    pot,
    pot_far,
    weight,
    weight_far,
    field,
    halo,
    far,
    layers,
    other,
    split,
    usplit,
    border,
    weighted,
    tile,
    slots,
    thin,
    in_sem,
    halo_send,
    halo_recv,
    far_send,
    far_recv,
    sib_send,
    sib_recv,
    red_send,
    red_recv,
    known,
):
    nx, nz, ny = rings
    doms = nx * nz * ny
    cells = doms * 8 * 8 * 128
    dom = lax.axis_index("dom")
    band = lax.axis_index("band")
    py = lax.rem(dom, ny)
    pz = lax.rem(lax.div(dom, ny), nz)
    px = lax.div(dom, ny * nz)
    left = lax.rem(dom + doms - 1, doms)
    right = lax.rem(dom + 1, doms)

    def at(x, z, y):
        return (x * nz + z) * ny + y

    pairs = nx // 2
    half = lax.div(px, 2)

    def member_yx(p):
        x = 2 * half + lax.rem(p, 2)
        return {"dom": at(x, pz, lax.div(p, 2)), "band": band}

    def member_core(p):
        return {**member_yx(lax.div(p, 2)), "band": lax.rem(p, 2)}

    def member_zx(p):
        x = jnp.where(lax.rem(p, pairs) == half, px, nx - 1 - px)
        return {"dom": at(x, lax.div(p, pairs), py), "band": band}

    place_yx = 2 * py + lax.rem(px, 2)
    along_z = (pairs * nz, pairs * pz + half, member_zx)
    sums = (
        (2 * ny, place_yx, member_yx, slots.at[0]),
        (*along_z, slots.at[1]),
        (4 * ny, 2 * place_yx + band, member_core, thin),
        (*along_z, slots.at[2]),
    )

    loads = [
        pltpu.make_async_copy(potential, pot, in_sem.at[2]),
        pltpu.make_async_copy(trial.at[pl.ds(0, 512)], nat.at[pl.ds(0, 512)], in_sem.at[0]),
        pltpu.make_async_copy(trial.at[pl.ds(512, 512)], nat.at[pl.ds(512, 512)], in_sem.at[1]),
    ]
    for load in loads:
        load.start()

    def along(axis, steps):
        where = [px, pz, py]
        size = rings[axis]
        where[axis] = lax.rem(where[axis] + steps + size, size)
        return {"dom": at(*where), "band": band}

    one_hop = [along(axis, way) for axis in range(3) for way in (1, -1)]
    two_hops = [
        along(axis, way)
        for axis in (1, 2)
        for way in (2, -2)
        if rings[axis] > 2
    ]
    sibling = {"dom": dom, "band": 1 - band}

    barrier = pltpu.get_barrier_semaphore()
    nearest = one_hop + [{"dom": d, "band": band} for d in (left, right)] + [sibling]
    for device in nearest:
        pl.semaphore_signal(barrier, inc=1, device_id=device, device_id_type=MESH)
    rounds = (one_hop, two_hops, two_hops, [sibling])

    def tell(r):
        for i, device in enumerate(rounds[r]):
            pl.semaphore_signal(
                known.at[r, i], inc=1, device_id=device, device_id_type=MESH
            )

    def hear(r):
        for i in range(len(rounds[r])):
            pl.semaphore_wait(known.at[r, i], 1)

    zeros = jnp.zeros((4, 8, 8, 128), jnp.float32)

    def clear(i, carry):
        s, g = lax.div(i, 2), lax.rem(i, 2)
        field[s, g, pl.ds(0, 4)] = zeros
        field[s, g, pl.ds(12, 4)] = zeros
        return carry

    def spread_weight(target, rows):
        rows = (rows + DIAG) * (1.0 / HALF_WIDTH)
        for y in range(8):
            target[y] = jnp.broadcast_to(rows[y : y + 1], (8, 128))

    def set_weight(x, carry):
        spread_weight(weight.at[x], pot[x])
        return carry

    def relayout(g):
        def body(x, carry):
            for y in range(8):
                field[0, g, 4 + x, y] = nat[pl.ds(g * 512 + x * 8 + y, 8, stride=64), :]
            return carry

        lax.fori_loop(0, 8, body, 0)

    has = (dom > 0, dom < doms - 1)

    def to_neighbour(side, src, dst, send_sem, recv_sem):
        return pltpu.make_async_remote_copy(
            src_ref=src,
            dst_ref=dst,
            send_sem=send_sem,
            recv_sem=recv_sem,
            device_id={"dom": right if side == 0 else left, "band": band},
            device_id_type=MESH,
        )

    def halo_copy(s, g, side, part):
        ys = pl.ds(part * YS, YS)
        return to_neighbour(
            side,
            field.at[s, g, pl.ds(8 if side == 0 else 4, 4), ys],
            halo.at[s, g, side, :, ys],
            halo_send.at[s, g, side, part],
            halo_recv.at[s, g, side, part],
        )

    def far_copy(g, side):
        return to_neighbour(
            side,
            field.at[last, g, pl.ds(6 if side == 0 else 8, 2)],
            far.at[g, side],
            far_send.at[g, side],
            far_recv.at[g, side],
        )

    def pot_copy(side):
        return to_neighbour(
            side,
            pot.at[pl.ds(6 if side == 0 else 0, 2)],
            pot_far.at[side],
            far_send.at[2, side],
            far_recv.at[2, side],
        )

    def send(side, copy):
        @pl.when(has[1 - side])
        def _():
            copy.start()

    lane = lax.broadcasted_iota(jnp.int32, (8, 8, 128), 2)

    def shifted_y(c, k):
        empty = jnp.zeros((k, 8, 128), jnp.float32)
        return jnp.concatenate([c[k:], empty], 0) + jnp.concatenate([empty, c[: 8 - k]], 0)

    def shifted_z(c, k):
        below = jnp.where(lane >= k, pltpu.roll(c, k, 2), 0.0)
        return below + jnp.where(lane < 128 - k, pltpu.roll(c, 128 - k, 2), 0.0)

    def local_part(s, g):
        def body(x, carry):
            c = field[s, g, 4 + x]
            total = weight[x] * c
            for k in range(1, 5):
                pairs = field[s, g, 4 + x + k] + field[s, g, 4 + x - k]
                pairs = pairs + shifted_y(c, k) + shifted_z(c, k)
                total = total + PAIR[k] * pairs
            if 1 <= s < DEGREE:
                total = 2.0 * total - field[s - 1, g, 4 + x]
            field[s + 1, g, 4 + x] = total
            return carry

        lax.fori_loop(0, 8, body, 0, unroll=True)

    def halo_part(s, g, side, part):
        twice = 1.0 if s == 0 else 2.0
        ys = pl.ds(part * YS, YS)
        cells_at = {n: halo[s, g, side, 4 - n if side == 0 else n - 1, ys] for n in range(1, 5)}
        for x in range(4):
            mine = 4 + x if side == 0 else 11 - x
            total = field[s + 1, g, mine, ys]
            for n in range(1, 5 - x):
                total = total + (twice * PAIR[x + n]) * cells_at[n]
            field[s + 1, g, mine, ys] = total

    def border_start(g, side):
        def cell(n):
            if n > 0:
                return halo[last, g, side, 4 - n if side == 0 else n - 1]
            return field[last, g, 4 - n if side == 0 else 11 + n]

        for n in (1, 2):
            c = cell(n)
            total = weight_far[side, 2 - n if side == 0 else n - 1] * c
            for k in range(1, 5):
                near = cell(n - k) + shifted_y(c, k) + shifted_z(c, k)
                if n + k < 5:
                    near = near + cell(n + k)
                total = total + PAIR[k] * near
            total = 2.0 * total - halo[last - 1, g, side, 4 - n if side == 0 else n - 1]
            layers[g, side, n - 1] = total

    def border_end(g, side):
        five, six = [far[g, side, 6 - n if side == 0 else n - 5] for n in (5, 6)]
        split_layer(side, 1, g, layers[g, side, 0] + (2.0 * PAIR[4]) * five)
        total = layers[g, side, 1] + (2.0 * PAIR[3]) * five
        split_layer(side, 2, g, total + (2.0 * PAIR[4]) * six)

    def sibling_copy(g, part):
        ys = pl.ds(part * YS, YS)
        return pltpu.make_async_remote_copy(
            src_ref=field.at[DEGREE, g, pl.ds(4, 8), ys],
            dst_ref=other.at[g, :, ys],
            send_sem=sib_send.at[g, part],
            recv_sem=sib_recv.at[g, part],
            device_id={"dom": dom, "band": 1 - band},
            device_id_type=MESH,
        )

    def sum_copy(f, d):
        count, place, member, into = sums[f]
        return pltpu.make_async_remote_copy(
            src_ref=into.at[place],
            dst_ref=into.at[place],
            send_sem=red_send.at[f],
            recv_sem=red_recv.at[f],
            device_id=member(lax.rem(place + d, count)),
            device_id_type=MESH,
        )

    def sum_start(f, value):
        count, place, _, into = sums[f]
        into[place] = value
        for d in far_first(count):
            sum_copy(f, d).start()

    def sum_tiles(f):
        count, place, member, into = sums[f]
        tiles = into.at[pl.ds(0, count - 1)]
        return pltpu.make_async_remote_copy(
            src_ref=tiles,
            dst_ref=tiles,
            send_sem=red_send.at[f],
            recv_sem=red_recv.at[f],
            device_id=member(lax.rem(place + 1, count)),
            device_id_type=MESH,
        )

    def summed(f):
        count, _, _, into = sums[f]
        sum_tiles(f).wait_recv()
        step = 2 if f == 2 else 1
        totals = []
        for first in range(step):
            total = into[first]
            for p in range(first + step, count, step):
                total = total + into[p]
            totals.append(total)
        return jnp.concatenate(totals, 0)

    def split_rows(value):
        high = value.astype(jnp.bfloat16).astype(jnp.float32)
        return jnp.concatenate([high, value - high], 0).astype(jnp.bfloat16)

    def lanes_at(x, y):
        return pl.ds(128 * (8 * YS * (y // YS) + YS * x + y % YS), 128)

    def split_into(target, first, ys, read):
        for x in range(8):
            for y in ys:
                target[pl.ds(first, 16), lanes_at(x, y)] = split_rows(read(x, y))

    own_rows = pl.multiple_of(band * 32, 32)
    other_rows = pl.multiple_of(32 - band * 32, 32)

    def of_part(part):
        return range(part * YS, (part + 1) * YS)

    def split_own(g, part):
        first = own_rows + 16 * g
        split_into(split, first, of_part(part), lambda x, y: field[DEGREE, g, 4 + x, y])

    def split_other(g, part):
        split_into(split, other_rows + 16 * g, of_part(part), lambda x, y: other[g, x, y])

    def product(left, right):
        return lax.dot_general(left, right, NT, preferred_element_type=jnp.float32)

    def gram_part(part, total):
        rows = split[:, pl.ds(part * YS * 1024, YS * 1024)]
        return total + product(rows, rows)

    def split_layer(side, n, g, value):
        for y in range(8):
            at_y = pl.ds(128 * (16 * side + 8 * n - 8 + y), 128)
            border[pl.ds(16 * g, 16), at_y] = split_rows(value[y])

    def weigh(first, read):
        for side in range(2):
            for n in (1, 2):
                for y in range(8):
                    total = None
                    for x in range(0 if side == 0 else 2, 5 - n):
                        value = (2.0 * PAIR[x + n]) * read(x if side == 0 else 7 - x, y)
                        total = value if total is None else total + value
                    at_y = pl.ds(128 * (16 * side + 8 * n - 8 + y), 128)
                    weighted[pl.ds(first, 16), at_y] = split_rows(total)

    def weigh_own(g):
        weigh(own_rows + 16 * g, lambda x, y: field[DEGREE, g, 4 + x, y])

    def weigh_other(g):
        weigh(other_rows + 16 * g, lambda x, y: other[g, x, y])

    def image_rows(g):
        local_part(DEGREE, g)
        split_into(usplit, 16 * g, range(8), lambda x, y: field[DEGREE + 1, g, 4 + x, y])
        weigh_own(g)
        for side in range(2):
            pl.when(has[side])(functools.partial(border_start, g, side))

    lanes = lax.broadcasted_iota(jnp.int32, (8, 128), 1)
    subs = lax.broadcasted_iota(jnp.int32, (8, 128), 0)
    used = (lanes < 64) & (lax.rem(lanes, 16) < 8)

    def folded(value):
        return value + pltpu.roll(value, 120, 1)

    def packed_gram(total):
        tile[:, pl.ds(0, 64)] = total
        value = jnp.zeros((8, 128), jnp.float32)
        for q in range(4):
            row = folded(tile[pl.ds(16 * q, 8)] + tile[pl.ds(16 * q + 8, 8)])
            row = jnp.where(used, row, 0.0)
            value = value + (row if q == 0 else pltpu.roll(row, SHIFT[q], 1))
        return value

    def unpacked_gram(value):
        rows = [value] + [pltpu.roll(value, 128 - SHIFT[q], 1) for q in range(1, 4)]
        return [jnp.where(used, row, 0.0) for row in rows]

    def packed_image(total):
        tile[pl.ds(0, 8), pl.ds(0, 64)] = total[:8] + total[8:16]
        tile[pl.ds(8, 8), pl.ds(0, 64)] = total[16:24] + total[24:]
        one, two = [jnp.where(used, folded(tile[pl.ds(8 * g, 8)]), 0.0) for g in range(2)]
        both = one + pltpu.roll(two, 8, 1)
        return (both + pltpu.roll(pltpu.roll(both, 64, 1), 4, 0))[:4]

    def unpacked_image(value):
        moved = pltpu.roll(value, 64, 1)
        one = jnp.where(subs < 4, value, pltpu.roll(moved, 4, 0))
        two = jnp.where(subs < 4, pltpu.roll(value, 4, 0), moved)
        rows = [one, pltpu.roll(one, 120, 1), two, pltpu.roll(two, 120, 1)]
        return [jnp.where(used, row, 0.0) for row in rows]

    last = DEGREE - 1

    for g in range(2):
        loads[1 + g].wait()
        relayout(g)
    pl.semaphore_wait(barrier, len(nearest))
    for g in range(2):
        for part in range(PARTS):
            for side in range(2):
                send(side, halo_copy(0, g, side, part))
    tell(0)
    loads[0].wait()
    for side in range(2):
        send(side, pot_copy(side))
    lax.fori_loop(0, 2 * (DEGREE + 1), clear, 0)
    tile[...] = jnp.zeros((64, 128), jnp.float32)
    lax.fori_loop(0, 8, set_weight, 0)
    for g in range(2):
        local_part(0, g)

    for s in range(last):
        for g in range(2):

            def exchange(part, carry):
                for side in range(2):

                    @pl.when(has[side])
                    def _():
                        halo_copy(s, g, side, part).wait_recv()
                        halo_part(s, g, side, part)
                        halo_copy(s + 1, g, 1 - side, part).start()

                return carry

            lax.fori_loop(0, PARTS, exchange, 0)
            local_part(s + 1, g)
        hear(s)
        tell(s + 1)
    for g in range(2):
        for side in range(2):
            send(side, far_copy(g, side))

    for side in range(2):

        @pl.when(has[side])
        def _():
            pot_copy(side).wait_recv()
            for n in range(2):
                spread_weight(weight_far.at[side, n], pot_far[side, n])

    gram = jnp.zeros((64, 64), jnp.float32)
    for g in range(2):
        for part in range(PARTS):
            for side in range(2):

                @pl.when(has[side])
                def _():
                    halo_copy(last, g, side, part).wait_recv()
                    halo_part(last, g, side, part)

            sibling_copy(g, part).start()
            split_own(g, part)
            if part > 0:
                sibling_copy(g, part - 1).wait_recv()
                split_other(g, part - 1)
                if g == 1:
                    gram = gram_part(part - 1, gram)
        image_rows(g)
        sibling_copy(g, PARTS - 1).wait_recv()
        split_other(g, PARTS - 1)
        if g == 0:
            weigh_other(0)
    hear(last)
    sum_start(0, packed_gram(gram_part(PARTS - 1, gram)))

    image = product(usplit[...], split[...])
    weigh_other(1)
    for g in range(2):
        for side in range(2):

            @pl.when(has[side])
            def _():
                far_copy(g, side).wait_recv()
                border_end(g, side)

    for side in range(2):

        @pl.when(jnp.logical_not(has[side]))
        def _():
            border[:, pl.ds(2048 * side, 2048)] = jnp.zeros((32, 2048), jnp.bfloat16)

    sum_start(2, packed_image(image + product(border[...], weighted[...])))
    sum_start(1, summed(0))
    sum_start(3, summed(2))

    gram = [row * (1.0 / cells) for row in unpacked_gram(summed(1))]
    rows = [jnp.where(lanes == subs + (64 + 16 * q), 1.0, gram[q]) for q in range(4)]
    inverse = eliminated(rows, subs)
    inverse = [jnp.where(used, pltpu.roll(row, 64, 1), 0.0) for row in inverse]

    own = [jnp.where(band == 0, inverse[q], inverse[2 + q]) for q in range(2)]
    own = split_rows(jnp.concatenate([v + pltpu.roll(v, 8, 1) for v in own], 0))[:, :64]

    outs = []
    for x in range(8):
        for part in range(PARTS):
            at_x = pl.ds(128 * YS * (8 * part + x), 128 * YS)
            value = lax.dot_general(own, split[:, at_x], NN, preferred_element_type=jnp.float32)
            value = value[:16] + value[16:]
            for y in range(YS):
                row = x // 4 * 512 + x % 4 * 8 + part * YS + y
                nat[pl.ds(row, 16, stride=32), :] = value[:, 128 * y : 128 * y + 128]
        if x % 4 == 3:
            rows_of = pl.ds(x // 4 * 512, 512)
            outs.append(pltpu.make_async_copy(nat.at[rows_of], orbitals.at[rows_of], in_sem.at[x // 4]))
            outs[-1].start()

    dot = functools.partial(
        lax.dot_general, precision=lax.Precision.HIGHEST, preferred_element_type=jnp.float32
    )
    inverse = jnp.concatenate(inverse, 0)[:, :64]
    column = lax.broadcasted_iota(jnp.int32, (64, 32), 1)
    spread = lax.broadcasted_iota(jnp.int32, (64, 32), 0)
    spread = spread == 16 * lax.div(column, 8) + lax.rem(column, 8)
    narrow = dot(inverse, jnp.where(spread, 1.0, 0.0), NN)
    for side in range(2):

        @pl.when(has[1 - side])
        def _():
            pot_copy(side).wait_send()
            for g in range(2):
                far_copy(g, side).wait_send()
                for s in range(DEGREE):
                    for part in range(PARTS):
                        halo_copy(s, g, side, part).wait_send()

    for g in range(2):
        for part in range(PARTS):
            sibling_copy(g, part).wait_send()
    for f in range(4):
        sum_tiles(f).wait_send()

    image = [(HALF_WIDTH / cells) * i + CENTER * g for i, g in zip(unpacked_image(summed(3)), gram)]
    image = jnp.concatenate(image, 0)[:, :64]
    one = dot(dot(narrow, image, NN), inverse, NT)
    two = dot(dot(inverse, image, NT), narrow, NT)
    projected[...] = 0.5 * (one + two)

    for out in outs:
        out.wait()


def eliminated(rows, subs):
    def spread(value):
        return jnp.broadcast_to(value, (8, 128))

    rows = list(rows)
    for r in range(4):
        lane = 16 * r
        column = {
            q: [spread(rows[q][:, lane + b : lane + b + 1]) for b in range(8)] for q in range(r, 4)
        }
        block = [[spread(column[r][b][a : a + 1]) for b in range(a + 1)] for a in range(8)]
        pivot = [spread(rows[r][a : a + 1]) for a in range(8)]
        factor = {q: [None] * 8 for q in range(r + 1, 4)}
        for k in range(8):
            reciprocal = 1.0 / block[k][k]
            for a in range(k + 1, 8):
                ratio = block[a][k] * reciprocal
                for b in range(k + 1, a + 1):
                    block[a][b] = block[a][b] - ratio * block[b][k]
                pivot[a] = pivot[a] - ratio * pivot[k]
            for q in range(r + 1, 4):
                factor[q][k] = column[q][k] * reciprocal
                for b in range(k + 1, 8):
                    column[q][b] = column[q][b] - factor[q][k] * block[b][k]
        for q in range(r + 1, 4):
            for k in range(8):
                rows[q] = rows[q] - factor[q][k] * pivot[k]
        done = pivot[0] * lax.rsqrt(block[0][0])
        for k in range(1, 8):
            done = jnp.where(subs == k, pivot[k] * lax.rsqrt(block[k][k]), done)
        rows[r] = done
    return rows


def hand_over(orbitals, projected, orbitals_out, projected_out, rows, matrix, read_sem, write_sem):
    steps = [(projected, matrix, projected_out)]
    for i in range(2):
        steps.append((orbitals.at[i], rows.at[i], orbitals_out.at[:, pl.ds(32 * i, 32)]))
    reads = [pltpu.make_async_copy(a, b, read_sem.at[i]) for i, (a, b, _) in enumerate(steps)]
    writes = [pltpu.make_async_copy(b, c, write_sem.at[i]) for i, (_, b, c) in enumerate(steps)]
    for read in reads:
        read.start()
    for read, write in zip(reads, writes):
        read.wait()
        write.start()
    for write in writes:
        write.wait()


def shards(trial_block, potential):
    rings = RINGS[lax.axis_size("dom")]
    most = max(2 * rings[2], rings[0] // 2 * rings[1])
    f32, dma = jnp.float32, pltpu.SemaphoreType.DMA
    orbitals, projected = pl.pallas_call(
        functools.partial(kernel, rings),
        out_shape=(
            jax.ShapeDtypeStruct((1024, 128), f32),
            jax.ShapeDtypeStruct((32, 32), f32),
        ),
        in_specs=[pl.BlockSpec(memory_space=pl.ANY)] * 2,
        out_specs=(
            pl.BlockSpec(memory_space=pl.ANY),
            pl.BlockSpec(memory_space=pltpu.VMEM),
        ),
        scratch_shapes=[
            pltpu.VMEM((1024, 128), f32),
            pltpu.VMEM((8, 8, 128), f32),
            pltpu.VMEM((2, 2, 8, 128), f32),
            pltpu.VMEM((8, 8, 8, 128), f32),
            pltpu.VMEM((2, 2, 8, 8, 128), f32),
            pltpu.VMEM((DEGREE + 2, 2, 16, 8, 8, 128), f32),
            pltpu.VMEM((DEGREE, 2, 2, 4, 8, 8, 128), f32),
            pltpu.VMEM((2, 2, 2, 8, 8, 128), f32),
            pltpu.VMEM((2, 2, 2, 8, 8, 128), f32),
            pltpu.VMEM((2, 8, 8, 8, 128), f32),
            pltpu.VMEM((64, 8192), jnp.bfloat16),
            pltpu.VMEM((32, 8192), jnp.bfloat16),
            pltpu.VMEM((32, 4096), jnp.bfloat16),
            pltpu.VMEM((64, 4096), jnp.bfloat16),
            pltpu.VMEM((64, 128), f32),
            pltpu.VMEM((3, most, 8, 128), f32),
            pltpu.VMEM((4 * rings[2], 4, 128), f32),
            dma((3,)),
            dma((DEGREE, 2, 2, PARTS)),
            dma((DEGREE, 2, 2, PARTS)),
            dma((3, 2)),
            dma((3, 2)),
            dma((2, PARTS)),
            dma((2, PARTS)),
            dma((4,)),
            dma((4,)),
            pltpu.SemaphoreType.REGULAR((4, 6)),
        ],
        compiler_params=pltpu.CompilerParams(
            collective_id=0, has_side_effects=True, vmem_limit_bytes=60 * 1024 * 1024
        ),
        cost_estimate=pl.CostEstimate(
            flops=200_000_000, bytes_accessed=1_100_000, transcendentals=0
        ),
    )(trial_block.reshape(1024, 128), potential)
    anywhere = pl.BlockSpec(memory_space=pl.ANY)
    orbitals, projected = pl.pallas_call(
        hand_over,
        out_shape=(
            jax.ShapeDtypeStruct((16, 64, 128), f32),
            jax.ShapeDtypeStruct((32, 32), f32),
        ),
        in_specs=[anywhere] * 2,
        out_specs=(anywhere, anywhere),
        scratch_shapes=[
            pltpu.VMEM((2, 16, 32, 128), f32),
            pltpu.VMEM((32, 32), f32),
            dma((3,)),
            dma((3,)),
        ],
        compiler_params=pltpu.CompilerParams(vmem_limit_bytes=60 * 1024 * 1024),
    )(orbitals.reshape(2, 16, 32, 128), projected)
    return orbitals.reshape(trial_block.shape), projected


def solution(mesh):
    return jax.shard_map(
        shards,
        mesh=mesh,
        in_specs=(P("band", "dom", None, None), P("dom", None, None)),
        out_specs=(P("band", "dom", None, None), P()),
        check_vma=False,
    )
```
